32 devices in a mesh: tracer: 4 (over z), gx: 2 (over x), gy: 4 (over y, core).
Axes of the slice: x: 2, y: 2, z: 4, core: 2. Of those that a mesh axis runs over, the one named last changes fastest.
Arguments:
- tracers: float32 [32, 4, 64, 512], P('tracer', None, 'gx', 'gy'), may hold values from -4 to 4
- air_mass: float32 [2, 4, 64, 512], P(None, 'tracer', 'gx', 'gy'), may hold values from 2 to 4
- flux_x: float32 [2, 4, 64, 512], P(None, 'tracer', 'gx', 'gy'), may hold values from -0.4 to 0.4
- flux_y: float32 [2, 4, 64, 512], P(None, 'tracer', 'gx', 'gy'), may hold values from -0.4 to 0.4
Outputs:
- advected: float32 [32, 4, 64, 512], P('tracer', None, 'gx', 'gy')
The draws below stay inside these ranges and needn't reach their ends.
All inputs are finite; a program needn't handle non-finite values.
Results may differ from the reference program's by a relative error of at most 0.0003.
Values sent between devices are 32-bit elements; how exact they have to be, the bound alone decides.
A program may use at most 64 MiB of HBM per device.

```python
import jax
import jax.numpy as jnp
from jax import lax

NTR = 32
LEV = 4
STEPS = 2
NX = 64
NY = 512


def level_of(key, dims, shards, smallest, high):
    gain = 1.0
    for position, blocks in shards:
        heights = jax.random.uniform(jax.random.fold_in(jax.random.fold_in(key, 6), position), (blocks,), jnp.float32, smallest / len(shards), high / len(shards))
        gain = gain * jnp.repeat(jnp.exp(heights), dims[position] // blocks).reshape((-1,) + (1,) * (len(dims) - 1 - position))
    return gain


def bell_draw(own_key, dims, scale, bound, pieces=(), held_as=jnp.bfloat16):
    result = scale * jax.random.normal(own_key, dims, jnp.float32)
    if pieces:
        result = result * level_of(own_key, dims, pieces, -0.22, 0.18)
    return jnp.clip(result, -bound, bound).astype(held_as)


def setup_inputs(seed: int = 0) -> dict:
    splits = jax.random.split(jax.random.key(seed), 5)
    tracers = bell_draw(splits[0], (NTR, LEV, NX, NY), 1.0, 4.0, ((0, 4), (2, 2), (3, 4)), jnp.float32)
    air_mass = jnp.clip(2.0 + 2.0 * jax.random.uniform(splits[1], (STEPS, LEV, NX, NY), jnp.float32) ** level_of(splits[1], (STEPS, LEV, NX, NY), ((1, 4), (2, 2), (3, 4)), -0.2, 0.2), 2.0, 4.0)
    flux_x = jnp.clip(jax.random.uniform(splits[2], (STEPS, LEV, NX, NY), jnp.float32, -0.4, 0.4) * level_of(splits[2], (STEPS, LEV, NX, NY), ((1, 4), (2, 2), (3, 4)), -0.4, 0.0), -0.4, 0.4)
    flux_y = jnp.clip(jax.random.uniform(splits[3], (STEPS, LEV, NX, NY), jnp.float32, -0.4, 0.4) * level_of(splits[3], (STEPS, LEV, NX, NY), ((1, 4), (2, 2), (3, 4)), -0.4, 0.0), -0.4, 0.4)
    return {"tracers": tracers, "air_mass": air_mass, "flux_x": flux_x, "flux_y": flux_y}


def window(array, begin_at, end_at, sweep_dim):
    return lax.slice_in_dim(array, begin_at, end_at, axis=array.ndim + sweep_dim)


def ppm_sweep(tracer_pad, mass_pad, faces, sweep_dim):
    length = tracer_pad.shape[sweep_dim] - 6
    far_left = window(tracer_pad, 0, length + 3, sweep_dim)
    near_left = window(tracer_pad, 1, length + 4, sweep_dim)
    near_right = window(tracer_pad, 2, length + 5, sweep_dim)
    far_right = window(tracer_pad, 3, length + 6, sweep_dim)
    edges = (7.0 / 12.0) * (near_left + near_right) - (1.0 / 12.0) * (far_left + far_right)
    edges = jnp.clip(edges, jnp.minimum(near_left, near_right), jnp.maximum(near_left, near_right))
    centre = window(tracer_pad, 2, length + 4, sweep_dim)
    left_edge = window(edges, 0, length + 2, sweep_dim)
    right_edge = window(edges, 1, length + 3, sweep_dim)
    extremum = (right_edge - centre) * (centre - left_edge) <= 0.0
    left_edge = jnp.where(extremum, centre, left_edge)
    right_edge = jnp.where(extremum, centre, right_edge)
    spread = right_edge - left_edge
    offset = centre - 0.5 * (left_edge + right_edge)
    steep_low = spread * offset > spread * spread / 6.0
    steep_high = -spread * spread / 6.0 > spread * offset
    new_left = jnp.where(steep_low, 3.0 * centre - 2.0 * right_edge, left_edge)
    new_right = jnp.where(steep_high, 3.0 * centre - 2.0 * left_edge, right_edge)
    spread = new_right - new_left
    curvature = 6.0 * (centre - 0.5 * (new_left + new_right))
    mass_cells = window(mass_pad, 2, length + 4, sweep_dim)
    courant_east = faces / window(mass_cells, 0, length + 1, sweep_dim)
    courant_west = -faces / window(mass_cells, 1, length + 2, sweep_dim)
    east_value = window(new_right, 0, length + 1, sweep_dim) - 0.5 * courant_east * (
        window(spread, 0, length + 1, sweep_dim)
        - (1.0 - (2.0 / 3.0) * courant_east) * window(curvature, 0, length + 1, sweep_dim))
    west_value = window(new_left, 1, length + 2, sweep_dim) + 0.5 * courant_west * (
        window(spread, 1, length + 2, sweep_dim)
        + (1.0 - (2.0 / 3.0) * courant_west) * window(curvature, 1, length + 2, sweep_dim))
    carried = faces * jnp.where(faces >= 0.0, east_value, west_value)
    mass_old = window(mass_pad, 3, length + 3, sweep_dim)
    tracer_old = window(tracer_pad, 3, length + 3, sweep_dim)
    mass_new = mass_old - (window(faces, 1, length + 1, sweep_dim) - window(faces, 0, length, sweep_dim))
    tracer_new = (mass_old * tracer_old
                  - (window(carried, 1, length + 1, sweep_dim) - window(carried, 0, length, sweep_dim))) / mass_new
    return tracer_new, mass_new


def reference(tracers, air_mass, flux_x, flux_y):
    def single(mixing):
        for substep in range(STEPS):
            air_now = air_mass[substep]
            east_flux = flux_x[substep]
            north_flux = flux_y[substep]
            tracer_pad = jnp.concatenate([mixing[:, -3:, :], mixing, mixing[:, :3, :]], axis=1)
            mass_pad = jnp.concatenate([air_now[:, -3:, :], air_now, air_now[:, :3, :]], axis=1)
            faces_east = jnp.concatenate([east_flux, east_flux[:, :1, :]], axis=1)
            after_east, mass_east = ppm_sweep(tracer_pad, mass_pad, faces_east, -2)
            tracer_pole = jnp.pad(after_east, ((0, 0), (0, 0), (3, 3)))
            mass_pole = jnp.pad(mass_east, ((0, 0), (0, 0), (3, 3)), constant_values=1.0)
            closed = jnp.zeros((north_flux.shape[0], north_flux.shape[1], 1), north_flux.dtype)
            faces_north = jnp.concatenate([closed, north_flux[:, :, 1:], closed], axis=2)
            mixing, mass_unused = ppm_sweep(tracer_pole, mass_pole, faces_north, -1)
        return mixing

    return lax.map(single, tracers)
```

```python
import functools

import jax
import jax.numpy as jnp
from jax import lax
from jax.experimental import pallas as pl
from jax.experimental.pallas import tpu as pltpu
from jax.sharding import PartitionSpec as P

MESH = pl.DeviceIdType.MESH
LANES = 128
SUB = 8


def sweep(q, face, cell, put, begin, end):
    steps, devs, limited, fluxes, rows = {}, {}, {}, {}, {}

    def Q(i):
        if i not in rows:
            rows[i] = q(i)
        return rows[i]

    def D(k):
        if k not in steps:
            steps[k] = Q(k) - Q(k - 1)
        return steps[k]

    def right_of(k):
        if k not in devs:
            raw = 0.5 * D(k) + (1.0 / 12.0) * (D(k - 1) - D(k + 1))
            devs[k] = jnp.minimum(jnp.maximum(raw, jnp.minimum(D(k), 0.0)), jnp.maximum(D(k), 0.0))
        return devs[k]

    def lim(i):
        if i not in limited:
            left, right = D(i) - right_of(i), right_of(i + 1)
            left2, right2 = left + left, right + right
            limited[i] = (
                jnp.minimum(jnp.maximum(left, jnp.minimum(right2, 0.0)), jnp.maximum(right2, 0.0)),
                jnp.minimum(jnp.maximum(right, jnp.minimum(left2, 0.0)), jnp.maximum(left2, 0.0)),
            )
        return limited[i]

    def G(k):
        if k not in fluxes:
            f, near_w, far_w = face(k)
            east = f >= 0.0
            (l0, r0), (l1, r1) = lim(k - 1), lim(k)
            fluxes[k] = (
                f * jnp.where(east, Q(k - 1), Q(k))
                + near_w * jnp.where(east, r0, l1)
                + far_w * jnp.where(east, l0, r1)
            )
        return fluxes[k]

    for i in range(begin, end):
        alpha, beta = cell(i)
        put(i, alpha * Q(i) - beta * (G(i + 1) - G(i)))


def face_weights(f, mass_left, mass_right):
    size = jnp.abs(f)
    c = size / jnp.where(f >= 0.0, mass_left, mass_right)
    rest = 1.0 - c
    part = size * rest
    return part * rest, part * c


def kernel(n_lev, n_x, n_y, steps, tl, nlon, x_ref, m_ref, fx_ref, fy_ref, o_ref,
           dyn, eout, ein, edge, hxo, hxi, hyo, hyi, xs, qx, yb, yo,
           cf, cp, cq, ca, cb, mp, fp, mxs, myp, fyp, yp, yq, ya, ybt,
           d_s, d_r, ea_s, ea_r, eb_s, eb_r, hx_s, hx_r, hy_s, hy_r):
    z, gx, gy = lax.axis_index("tracer"), lax.axis_index("gx"), lax.axis_index("gy")
    peers = [lax.rem(z + d, n_lev) for d in range(1, n_lev)]
    left, right = lax.rem(gx + n_x - 1, n_x), lax.rem(gx + 1, n_x)
    south, north = lax.rem(gy + n_y - 1, n_y), lax.rem(gy + 1, n_y)
    H = 3
    nl = n_lev * nlon

    barrier = pltpu.get_barrier_semaphore()
    who = [{"tracer": p} for p in peers] + [{"gx": left}, {"gx": right}, {"gy": south}, {"gy": north}]
    for w in who:
        pl.semaphore_signal(barrier, inc=1, device_id=w, device_id_type=MESH)

    def remote(src, dst, ss, rs, to):
        return pltpu.make_async_remote_copy(src_ref=src, dst_ref=dst, send_sem=ss, recv_sem=rs,
                                            device_id=to, device_id_type=MESH)

    def pack_x(s, src):
        def body(lev, _):
            for c in range(H):
                to = pl.ds(pl.multiple_of((lev * H + c) * SUB, SUB), SUB)
                hxo[s, 0, to, :] = src[pl.ds(lev * nlon + c, SUB, stride=nl), :]
                hxo[s, 1, to, :] = src[pl.ds(lev * nlon + nlon - H + c, SUB, stride=nl), :]
            return 0
        lax.fori_loop(0, n_lev, body, 0)

    for s in range(steps):
        for f, ref in enumerate((m_ref, fx_ref, fy_ref)):
            dyn[s * n_lev + z, f * nlon:(f + 1) * nlon, :] = ref[s * nlon:(s + 1) * nlon, :]
        eout[s * 4:s * 4 + 1, :] = m_ref[(s + 1) * nlon - 1:(s + 1) * nlon, :]
        eout[s * 4 + 1:s * 4 + 2, :] = m_ref[s * nlon:s * nlon + 1, :]
        eout[s * 4 + 2:s * 4 + 3, :] = fx_ref[s * nlon:s * nlon + 1, :]
        eout[s * 4 + 3:s * 4 + 4, :] = fx_ref[s * nlon:s * nlon + 1, :]
    pack_x(0, x_ref)
    pl.semaphore_wait(barrier, len(who))

    pending = []

    def go(copy):
        copy.start()
        pending.append(copy)

    go(remote(eout, ein.at[1], ea_s.at[0], ea_r.at[1], {"gx": left}))
    go(remote(eout, ein.at[0], ea_s.at[1], ea_r.at[0], {"gx": right}))

    def send_dyn(s):
        for d, p in enumerate(peers):
            go(remote(dyn.at[s * n_lev + z], dyn.at[s * n_lev + z], d_s.at[s, d], d_r.at[s, z], {"tracer": p}))

    def send_x(s):
        go(remote(hxo.at[s, 0], hxi.at[s, 1], hx_s.at[s, 0], hx_r.at[s, 1], {"gx": left}))
        go(remote(hxo.at[s, 1], hxi.at[s, 0], hx_s.at[s, 1], hx_r.at[s, 0], {"gx": right}))

    send_dyn(0)
    send_x(0)
    for side in range(2):
        remote(eout, ein.at[side], ea_s.at[side], ea_r.at[side], {"gx": left}).wait_recv()
    for s in range(steps):
        edge[z, s * 4:s * 4 + 1, :] = ein[0, s * 4:s * 4 + 1, :]
        edge[z, s * 4 + 1:s * 4 + 4, :] = ein[1, s * 4 + 1:s * 4 + 4, :]
    for d, p in enumerate(peers):
        go(remote(edge.at[z], edge.at[z], eb_s.at[d], eb_r.at[z], {"tracer": p}))
    for s in range(1, steps):
        send_dyn(s)

    for s in range(steps):
        src = x_ref if s == 0 else xs
        dst = xs if s < steps - 1 else o_ref

        def x_inner(j, _):
            lev = lax.rem(z + j, n_lev)
            slot = s * n_lev + lev

            @pl.when(j > 0)
            def _():
                remote(dyn.at[slot], dyn.at[slot], d_s.at[s, 0], d_r.at[s, lev], {"tracer": z}).wait_recv()
                if s == 0:
                    remote(edge.at[lev], edge.at[lev], eb_s.at[0], eb_r.at[lev], {"tracer": z}).wait_recv()

            m = dyn[slot, 0:nlon, :]
            mp[SUB:SUB + nlon, :] = m
            mp[0:SUB, :] = jnp.broadcast_to(edge[lev, s * 4:s * 4 + 1, :], (SUB, LANES))
            mp[SUB + nlon:2 * SUB + nlon, :] = jnp.broadcast_to(edge[lev, s * 4 + 1:s * 4 + 2, :], (SUB, LANES))
            fp[0:nlon, :] = dyn[slot, nlon:2 * nlon, :]
            fp[nlon:nlon + SUB, :] = jnp.broadcast_to(edge[lev, s * 4 + 2:s * 4 + 3, :], (SUB, LANES))
            f = fp[0:nlon + SUB, :]
            pw, qw = face_weights(f, mp[SUB - 1:2 * SUB - 1 + nlon, :], mp[SUB:2 * SUB + nlon, :])
            cf[lev] = f
            cp[lev] = pw
            cq[lev] = qw
            mx = m - (fp[1:nlon + 1, :] - fp[0:nlon, :])
            inv = 1.0 / mx
            ca[lev] = m * inv
            cb[lev] = inv
            mxs[pl.ds(pl.multiple_of(lev * nlon, nlon), nlon), :] = mx
            base = lev * nlon
            sweep(
                lambda i: src[pl.ds(base + i, SUB, stride=nl), :],
                lambda k: (cf[lev, k:k + 1, :], cp[lev, k:k + 1, :], cq[lev, k:k + 1, :]),
                lambda i: (ca[lev, i:i + 1, :], cb[lev, i:i + 1, :]),
                functools.partial(put_x, base), H, nlon - H)
            return 0

        def put_x(base, i, v):
            qx[pl.ds(base + i, SUB, stride=nl), :] = v

        lax.fori_loop(0, n_lev, x_inner, 0)
        for side in range(2):
            remote(hxo.at[s, 0], hxi.at[s, side], hx_s.at[s, side], hx_r.at[s, side], {"gx": left}).wait_recv()

        def x_edge(lev, _):
            base = lev * nlon

            def q(i):
                if i < 0:
                    return hxi[s, 0, pl.ds(pl.multiple_of((lev * H + i + H) * SUB, SUB), SUB), :]
                if i >= nlon:
                    return hxi[s, 1, pl.ds(pl.multiple_of((lev * H + i - nlon) * SUB, SUB), SUB), :]
                return src[pl.ds(base + i, SUB, stride=nl), :]

            for a, b in ((0, H), (nlon - H, nlon)):
                sweep(
                    q,
                    lambda k: (cf[lev, k:k + 1, :], cp[lev, k:k + 1, :], cq[lev, k:k + 1, :]),
                    lambda i: (ca[lev, i:i + 1, :], cb[lev, i:i + 1, :]),
                    functools.partial(put_x, base), a, b)
            return 0

        lax.fori_loop(0, n_lev, x_edge, 0)

        off = H * SUB

        def turn(t, _):
            yb[pl.ds(off + t, LANES, stride=SUB), :] = jnp.transpose(
                qx[pl.ds(pl.multiple_of(t * nl, nl), nl), :])
            return 0
        lax.fori_loop(0, SUB, turn, 0)
        mt = jnp.transpose(mxs[...])
        ft = jnp.transpose(jnp.concatenate(
            [dyn[s * n_lev + lev, 2 * nlon:3 * nlon, :] for lev in range(n_lev)], axis=0))
        myp[SUB:SUB + LANES, :] = mt
        fyp[0:LANES, :] = ft
        extra = jnp.concatenate([mt[0:1], mt[LANES - 1:LANES], ft[0:1], ft[0:1], ft[0:1], ft[0:1], ft[0:1], ft[0:1]], axis=0)
        for side in range(2):
            hyo[s, side, H * SUB:(H + 1) * SUB, :] = extra
        hyo[s, 0, 0:H * SUB, :] = yb[off:off + H * SUB, :]
        hyo[s, 1, 0:H * SUB, :] = yb[off + (LANES - H) * SUB:off + LANES * SUB, :]
        go(remote(hyo.at[s, 0], hyi.at[s, 1], hy_s.at[s, 0], hy_r.at[s, 1], {"gy": south}))
        go(remote(hyo.at[s, 1], hyi.at[s, 0], hy_s.at[s, 1], hy_r.at[s, 0], {"gy": north}))

        f = fyp[SUB:LANES, :]
        pw, qw = face_weights(f, myp[2 * SUB - 1:SUB + LANES - 1, :], myp[2 * SUB:SUB + LANES, :])
        yp[SUB:LANES, :] = pw
        yq[SUB:LANES, :] = qw
        m = myp[SUB:LANES, :]
        inv = 1.0 / (m - (fyp[1:LANES - SUB + 1, :] - fyp[0:LANES - SUB, :]))
        ya[0:LANES - SUB, :] = m * inv
        ybt[0:LANES - SUB, :] = inv

        def y_rows(first, count):
            sweep(
                lambda i: yb[pl.ds(pl.multiple_of(off + (first + i) * SUB, SUB), SUB), :],
                lambda k: (fyp[pl.ds(first + k, 1), :], yp[pl.ds(first + k, 1), :], yq[pl.ds(first + k, 1), :]),
                lambda i: (ya[pl.ds(first + i, 1), :], ybt[pl.ds(first + i, 1), :]),
                put_y(first), 0, count)

        def put_y(first):
            def put(i, v):
                yo[pl.ds(pl.multiple_of((first + i) * SUB, SUB), SUB), :] = v
            return put

        def y_inner(b, _):
            y_rows(SUB + b * 16, 16)
            return 0
        lax.fori_loop(0, (LANES - 2 * SUB) // 16, y_inner, 0)

        for side in range(2):
            remote(hyo.at[s, 0], hyi.at[s, side], hy_s.at[s, side], hy_r.at[s, side], {"gy": south}).wait_recv()
        at_south, at_north = gy == 0, gy == n_y - 1
        yb[0:H * SUB, :] = jnp.where(at_south, 0.0, hyi[s, 0, 0:H * SUB, :])
        yb[off + LANES * SUB:off + (LANES + H) * SUB, :] = jnp.where(at_north, 0.0, hyi[s, 1, 0:H * SUB, :])
        e = H * SUB
        myp[0:SUB, :] = jnp.broadcast_to(jnp.where(at_south, 1.0, hyi[s, 0, e + 1:e + 2, :]), (SUB, LANES))
        myp[SUB + LANES:2 * SUB + LANES, :] = jnp.broadcast_to(
            jnp.where(at_north, 1.0, hyi[s, 1, e:e + 1, :]), (SUB, LANES))
        fyp[LANES:LANES + SUB, :] = jnp.broadcast_to(
            jnp.where(at_north, 0.0, hyi[s, 1, e + 2:e + 3, :]), (SUB, LANES))
        fyp[0:1, :] = jnp.where(at_south, 0.0, fyp[0:1, :])
        for a in (0, LANES):
            f = fyp[a:a + SUB, :]
            pw, qw = face_weights(f, myp[a + SUB - 1:a + 2 * SUB - 1, :], myp[a + SUB:a + 2 * SUB, :])
            yp[a:a + SUB, :] = pw
            yq[a:a + SUB, :] = qw
        for a in (0, LANES - SUB):
            m = myp[a + SUB:a + 2 * SUB, :]
            inv = 1.0 / (m - (fyp[a + 1:a + SUB + 1, :] - fyp[a:a + SUB, :]))
            ya[a:a + SUB, :] = m * inv
            ybt[a:a + SUB, :] = inv

        def y_edge(b, _):
            y_rows(b * (LANES - SUB), SUB)
            return 0
        lax.fori_loop(0, 2, y_edge, 0)

        def back(t, _):
            dst[pl.ds(pl.multiple_of(t * nl, nl), nl), :] = jnp.transpose(yo[pl.ds(t, LANES, stride=SUB), :])
            return 0
        lax.fori_loop(0, SUB, back, 0)
        if s < steps - 1:
            pack_x(s + 1, xs)
            send_x(s + 1)

    for copy in pending:
        copy.wait_send()


def on_device(tracers, air_mass, flux_x, flux_y):
    nt, nlev, nlon, nlat = tracers.shape
    steps, tl = air_mass.shape[:2]
    n_lev, n_x, n_y = lax.axis_size("tracer"), lax.axis_size("gx"), lax.axis_size("gy")
    assert nt == SUB and nlat == LANES and nlev * nlon == LANES and tl == 1 and steps * 4 <= SUB
    rows = nt * nlev * nlon
    V = lambda *shape: pltpu.VMEM(shape, jnp.float32)
    dma = lambda *shape: pltpu.SemaphoreType.DMA(shape)
    H = 3
    out = pl.pallas_call(
        functools.partial(kernel, n_lev, n_x, n_y, steps, tl, nlon),
        out_shape=jax.ShapeDtypeStruct((rows, LANES), jnp.float32),
        in_specs=[pl.BlockSpec(memory_space=pltpu.VMEM)] * 4,
        out_specs=pl.BlockSpec(memory_space=pltpu.VMEM),
        scratch_shapes=[
            V(steps * n_lev, 3 * nlon, LANES),
            V(SUB, LANES), V(2, SUB, LANES), V(n_lev, SUB, LANES),
            V(steps, 2, n_lev * H * SUB, LANES), V(steps, 2, n_lev * H * SUB, LANES),
            V(steps, 2, (H + 1) * SUB, LANES), V(steps, 2, (H + 1) * SUB, LANES),
            V(rows, LANES), V(rows, LANES), V((LANES + 2 * H) * SUB, LANES), V(LANES * SUB, LANES),
            V(n_lev, nlon + SUB, LANES), V(n_lev, nlon + SUB, LANES), V(n_lev, nlon + SUB, LANES),
            V(n_lev, nlon, LANES), V(n_lev, nlon, LANES),
            V(nlon + 2 * SUB, LANES), V(nlon + SUB, LANES), V(LANES, LANES),
            V(LANES + 2 * SUB, LANES), V(LANES + SUB, LANES), V(LANES + SUB, LANES), V(LANES + SUB, LANES),
            V(LANES, LANES), V(LANES, LANES),
            dma(steps, n_lev), dma(steps, n_lev), dma(2), dma(2), dma(n_lev), dma(n_lev),
            dma(steps, 2), dma(steps, 2), dma(steps, 2), dma(steps, 2),
        ],
        compiler_params=pltpu.CompilerParams(
            collective_id=0, has_side_effects=True, vmem_limit_bytes=32 * 1024 * 1024),
    )(tracers.reshape(rows, LANES), air_mass.reshape(-1, LANES), flux_x.reshape(-1, LANES), flux_y.reshape(-1, LANES))
    return out.reshape(tracers.shape)


def solution(mesh):
    in_specs = (
        P("tracer", None, "gx", "gy"),
        P(None, "tracer", "gx", "gy"),
        P(None, "tracer", "gx", "gy"),
        P(None, "tracer", "gx", "gy"),
    )
    out_specs = P("tracer", None, "gx", "gy")
    return jax.shard_map(
        on_device, mesh=mesh, in_specs=in_specs, out_specs=out_specs, check_vma=False
    )
```

```python
import functools

import jax
import jax.numpy as jnp
from jax import lax
from jax.experimental import pallas as pl
from jax.experimental.pallas import tpu as pltpu
from jax.sharding import PartitionSpec as P

MESH = pl.DeviceIdType.MESH
LANES = 128
SUB = 8


def sweep(q, face, cell, put, begin, end):
    steps, devs, limited, fluxes, rows = {}, {}, {}, {}, {}

    def Q(i):
        if i not in rows:
            rows[i] = q(i)
        return rows[i]

    def D(k):
        if k not in steps:
            steps[k] = Q(k) - Q(k - 1)
        return steps[k]

    def right_of(k):
        if k not in devs:
            raw = 0.5 * D(k) + (1.0 / 12.0) * (D(k - 1) - D(k + 1))
            devs[k] = jnp.minimum(jnp.maximum(raw, jnp.minimum(D(k), 0.0)), jnp.maximum(D(k), 0.0))
        return devs[k]

    def lim(i):
        if i not in limited:
            left, right = D(i) - right_of(i), right_of(i + 1)
            left2, right2 = left + left, right + right
            limited[i] = (
                jnp.minimum(jnp.maximum(left, jnp.minimum(right2, 0.0)), jnp.maximum(right2, 0.0)),
                jnp.minimum(jnp.maximum(right, jnp.minimum(left2, 0.0)), jnp.maximum(left2, 0.0)),
            )
        return limited[i]

    def G(k):
        if k not in fluxes:
            f, near_w, far_w = face(k)
            east = f >= 0.0
            (l0, r0), (l1, r1) = lim(k - 1), lim(k)
            fluxes[k] = (
                f * jnp.where(east, Q(k - 1), Q(k))
                + near_w * jnp.where(east, r0, l1)
                + far_w * jnp.where(east, l0, r1)
            )
        return fluxes[k]

    for i in range(begin, end):
        alpha, beta = cell(i)
        put(i, alpha * Q(i) - beta * (G(i + 1) - G(i)))


def face_weights(f, mass_left, mass_right):
    size = jnp.abs(f)
    c = size / jnp.where(f >= 0.0, mass_left, mass_right)
    rest = 1.0 - c
    part = size * rest
    return part * rest, part * c


def kernel(n_lev, n_x, n_y, steps, tl, nlon, x_hbm, m_ref, fx_ref, fy_ref, o_ref,
           x_ref, in_sem, dyn, eout, ein, edge, hxo, hxi, hyo, hyi, xs, qx, yb, yo,
           cf, cp, cq, ca, cb, mp, fp, mxs, myp, fyp, yp, yq, ya, ybt,
           d_s, d_r, ea_s, ea_r, eb_s, eb_r, hx_s, hx_r, hy_s, hy_r):
    z, gx, gy = lax.axis_index("tracer"), lax.axis_index("gx"), lax.axis_index("gy")
    peers = [lax.rem(z + d, n_lev) for d in range(1, n_lev)]
    left, right = lax.rem(gx + n_x - 1, n_x), lax.rem(gx + 1, n_x)
    south, north = lax.rem(gy + n_y - 1, n_y), lax.rem(gy + 1, n_y)
    H = 3
    nl = n_lev * nlon

    barrier = pltpu.get_barrier_semaphore()
    who = [{"tracer": p} for p in peers] + [{"gx": left}, {"gx": right}, {"gy": south}, {"gy": north}]
    for w in who:
        pl.semaphore_signal(barrier, inc=1, device_id=w, device_id_type=MESH)

    def remote(src, dst, ss, rs, to):
        return pltpu.make_async_remote_copy(src_ref=src, dst_ref=dst, send_sem=ss, recv_sem=rs,
                                            device_id=to, device_id_type=MESH)

    loads = []
    for s in range(steps):
        for f, ref in enumerate((m_ref, fx_ref, fy_ref)):
            loads.append(pltpu.make_async_copy(
                ref.at[pl.ds(s * nlon, nlon)], dyn.at[s * n_lev + z, pl.ds(f * nlon, nlon)], in_sem.at[len(loads)]))
            loads[-1].start()
    load_x = pltpu.make_async_copy(x_hbm, x_ref, in_sem.at[len(loads)])
    load_x.start()

    def pack_x(s, src):
        def body(lev, _):
            for c in range(H):
                to = pl.ds(pl.multiple_of((lev * H + c) * SUB, SUB), SUB)
                hxo[s, 0, to, :] = src[pl.ds(lev * nlon + c, SUB, stride=nl), :]
                hxo[s, 1, to, :] = src[pl.ds(lev * nlon + nlon - H + c, SUB, stride=nl), :]
            return 0
        lax.fori_loop(0, n_lev, body, 0)

    for copy in loads:
        copy.wait()
    for s in range(steps):
        own = s * n_lev + z
        eout[s * 4:s * 4 + 1, :] = dyn[own, nlon - 1:nlon, :]
        eout[s * 4 + 1:s * 4 + 2, :] = dyn[own, 0:1, :]
        eout[s * 4 + 2:s * 4 + 3, :] = dyn[own, nlon:nlon + 1, :]
        eout[s * 4 + 3:s * 4 + 4, :] = dyn[own, nlon:nlon + 1, :]
    mp[0:SUB, :] = jnp.ones((SUB, LANES), jnp.float32)
    fp[nlon:nlon + SUB, :] = jnp.zeros((SUB, LANES), jnp.float32)
    load_x.wait()
    pack_x(0, x_ref)
    pl.semaphore_wait(barrier, len(who))

    pending = []

    def go(copy):
        copy.start()
        pending.append(copy)

    go(remote(eout, ein.at[1], ea_s.at[0], ea_r.at[1], {"gx": left}))
    go(remote(eout, ein.at[0], ea_s.at[1], ea_r.at[0], {"gx": right}))

    def send_dyn(s):
        for d, p in enumerate(peers):
            go(remote(dyn.at[s * n_lev + z], dyn.at[s * n_lev + z], d_s.at[s, d], d_r.at[s, z], {"tracer": p}))

    def send_x(s):
        go(remote(hxo.at[s, 0], hxi.at[s, 1], hx_s.at[s, 0], hx_r.at[s, 1], {"gx": left}))
        go(remote(hxo.at[s, 1], hxi.at[s, 0], hx_s.at[s, 1], hx_r.at[s, 0], {"gx": right}))

    send_x(0)
    send_dyn(0)

    def share_edges():
        for side in range(2):
            remote(eout, ein.at[side], ea_s.at[side], ea_r.at[side], {"gx": left}).wait_recv()
        for s in range(steps):
            edge[z, s * 4:s * 4 + 1, :] = ein[0, s * 4:s * 4 + 1, :]
            edge[z, s * 4 + 1:s * 4 + 4, :] = ein[1, s * 4 + 1:s * 4 + 4, :]
        for d, p in enumerate(peers):
            go(remote(edge.at[z], edge.at[z], eb_s.at[d], eb_r.at[z], {"tracer": p}))

    for s in range(steps):
        src = x_ref if s == 0 else xs
        dst = xs if s < steps - 1 else o_ref

        def x_inner(j, _):
            lev = lax.rem(z + j, n_lev)
            slot = s * n_lev + lev

            def here():
                remote(dyn.at[slot], dyn.at[slot], d_s.at[s, 0], d_r.at[s, lev], {"tracer": z}).wait_recv()
            if s > 0:
                pl.when(j > 0)(here)
            elif not isinstance(j, int):
                here()

            m = dyn[slot, 0:nlon, :]
            mp[SUB:SUB + nlon, :] = m
            fp[0:nlon, :] = dyn[slot, nlon:2 * nlon, :]
            f = fp[0:nlon, :]
            pw, qw = face_weights(f, mp[SUB - 1:SUB - 1 + nlon, :], m)
            cf[lev, 0:nlon, :] = f
            cp[lev, 0:nlon, :] = pw
            cq[lev, 0:nlon, :] = qw
            mx = m - (fp[1:nlon + 1, :] - f)
            inv = 1.0 / mx
            ca[lev] = m * inv
            cb[lev] = inv
            mxs[pl.ds(pl.multiple_of(lev * nlon, nlon), nlon), :] = mx
            base = lev * nlon
            sweep(
                lambda i: src[pl.ds(base + i, SUB, stride=nl), :],
                lambda k: (cf[lev, k:k + 1, :], cp[lev, k:k + 1, :], cq[lev, k:k + 1, :]),
                lambda i: (ca[lev, i:i + 1, :], cb[lev, i:i + 1, :]),
                functools.partial(put_x, base), H, nlon - H)
            return 0

        def put_x(base, i, v):
            qx[pl.ds(base + i, SUB, stride=nl), :] = v

        if s == 0:
            x_inner(0, 0)
            share_edges()
            lax.fori_loop(1, n_lev, x_inner, 0)

            def edge_here(j, _):
                lev = lax.rem(z + j, n_lev)
                remote(edge.at[lev], edge.at[lev], eb_s.at[0], eb_r.at[lev], {"tracer": z}).wait_recv()
                return 0
            lax.fori_loop(1, n_lev, edge_here, 0)
            for later in range(1, steps):
                send_dyn(later)
        else:
            lax.fori_loop(0, n_lev, x_inner, 0)
        for side in range(2):
            remote(hxo.at[s, 0], hxi.at[s, side], hx_s.at[s, side], hx_r.at[s, side], {"gx": left}).wait_recv()

        def x_edge(lev, _):
            base = lev * nlon
            slot = s * n_lev + lev
            first = slice(nlon, nlon + 1)
            m_w = edge[lev, s * 4:s * 4 + 1, :]
            m_e = edge[lev, s * 4 + 1:s * 4 + 2, :]
            f_e = edge[lev, s * 4 + 2:s * 4 + 3, :]
            f_w = dyn[slot, first, :]
            pw, qw = face_weights(f_w, m_w, dyn[slot, 0:1, :])
            cp[lev, 0:1, :] = pw
            cq[lev, 0:1, :] = qw
            m_last = dyn[slot, nlon - 1:nlon, :]
            pw, qw = face_weights(f_e, m_last, m_e)
            cf[lev, first, :] = f_e
            cp[lev, first, :] = pw
            cq[lev, first, :] = qw
            mx = m_last - (f_e - dyn[slot, 2 * nlon - 1:2 * nlon, :])
            inv = 1.0 / mx
            ca[lev, nlon - 1:nlon, :] = m_last * inv
            cb[lev, nlon - 1:nlon, :] = inv
            mxs[pl.ds(base + nlon - 1, 1), :] = mx

            def q(i):
                if i < 0:
                    return hxi[s, 0, pl.ds(pl.multiple_of((lev * H + i + H) * SUB, SUB), SUB), :]
                if i >= nlon:
                    return hxi[s, 1, pl.ds(pl.multiple_of((lev * H + i - nlon) * SUB, SUB), SUB), :]
                return src[pl.ds(base + i, SUB, stride=nl), :]

            for a, b in ((0, H), (nlon - H, nlon)):
                sweep(
                    q,
                    lambda k: (cf[lev, k:k + 1, :], cp[lev, k:k + 1, :], cq[lev, k:k + 1, :]),
                    lambda i: (ca[lev, i:i + 1, :], cb[lev, i:i + 1, :]),
                    functools.partial(put_x, base), a, b)
            return 0

        lax.fori_loop(0, n_lev, x_edge, 0)

        off = H * SUB

        def turn(t, _):
            yb[pl.ds(off + t, LANES, stride=SUB), :] = jnp.transpose(
                qx[pl.ds(pl.multiple_of(t * nl, nl), nl), :])
            return 0
        lax.fori_loop(0, SUB, turn, 0, unroll=True)
        mt = jnp.transpose(mxs[...])
        ft = jnp.transpose(jnp.concatenate(
            [dyn[s * n_lev + lev, 2 * nlon:3 * nlon, :] for lev in range(n_lev)], axis=0))
        myp[SUB:SUB + LANES, :] = mt
        fyp[0:LANES, :] = ft
        extra = jnp.concatenate([mt[0:1], mt[LANES - 1:LANES], ft[0:1], ft[0:1], ft[0:1], ft[0:1], ft[0:1], ft[0:1]], axis=0)
        for side in range(2):
            hyo[s, side, H * SUB:(H + 1) * SUB, :] = extra
        hyo[s, 0, 0:H * SUB, :] = yb[off:off + H * SUB, :]
        hyo[s, 1, 0:H * SUB, :] = yb[off + (LANES - H) * SUB:off + LANES * SUB, :]
        go(remote(hyo.at[s, 0], hyi.at[s, 1], hy_s.at[s, 0], hy_r.at[s, 1], {"gy": south}))
        go(remote(hyo.at[s, 1], hyi.at[s, 0], hy_s.at[s, 1], hy_r.at[s, 0], {"gy": north}))

        f = fyp[SUB:LANES, :]
        pw, qw = face_weights(f, myp[2 * SUB - 1:SUB + LANES - 1, :], myp[2 * SUB:SUB + LANES, :])
        yp[SUB:LANES, :] = pw
        yq[SUB:LANES, :] = qw
        m = myp[SUB:LANES, :]
        inv = 1.0 / (m - (fyp[1:LANES - SUB + 1, :] - fyp[0:LANES - SUB, :]))
        ya[0:LANES - SUB, :] = m * inv
        ybt[0:LANES - SUB, :] = inv

        def y_rows(first, count):
            sweep(
                lambda i: yb[pl.ds(pl.multiple_of(off + (first + i) * SUB, SUB), SUB), :],
                lambda k: (fyp[pl.ds(first + k, 1), :], yp[pl.ds(first + k, 1), :], yq[pl.ds(first + k, 1), :]),
                lambda i: (ya[pl.ds(first + i, 1), :], ybt[pl.ds(first + i, 1), :]),
                put_y(first), 0, count)

        def put_y(first):
            def put(i, v):
                yo[pl.ds(pl.multiple_of((first + i) * SUB, SUB), SUB), :] = v
            return put

        def y_inner(b, _):
            y_rows(SUB + b * 16, 16)
            return 0
        lax.fori_loop(0, (LANES - 2 * SUB) // 16, y_inner, 0)

        for side in range(2):
            remote(hyo.at[s, 0], hyi.at[s, side], hy_s.at[s, side], hy_r.at[s, side], {"gy": south}).wait_recv()
        at_south, at_north = gy == 0, gy == n_y - 1
        yb[0:H * SUB, :] = jnp.where(at_south, 0.0, hyi[s, 0, 0:H * SUB, :])
        yb[off + LANES * SUB:off + (LANES + H) * SUB, :] = jnp.where(at_north, 0.0, hyi[s, 1, 0:H * SUB, :])
        e = H * SUB
        myp[0:SUB, :] = jnp.broadcast_to(jnp.where(at_south, 1.0, hyi[s, 0, e + 1:e + 2, :]), (SUB, LANES))
        myp[SUB + LANES:2 * SUB + LANES, :] = jnp.broadcast_to(
            jnp.where(at_north, 1.0, hyi[s, 1, e:e + 1, :]), (SUB, LANES))
        fyp[LANES:LANES + SUB, :] = jnp.broadcast_to(
            jnp.where(at_north, 0.0, hyi[s, 1, e + 2:e + 3, :]), (SUB, LANES))
        fyp[0:1, :] = jnp.where(at_south, 0.0, fyp[0:1, :])
        for a in (0, LANES):
            f = fyp[a:a + SUB, :]
            pw, qw = face_weights(f, myp[a + SUB - 1:a + 2 * SUB - 1, :], myp[a + SUB:a + 2 * SUB, :])
            yp[a:a + SUB, :] = pw
            yq[a:a + SUB, :] = qw
        for a in (0, LANES - SUB):
            m = myp[a + SUB:a + 2 * SUB, :]
            inv = 1.0 / (m - (fyp[a + 1:a + SUB + 1, :] - fyp[a:a + SUB, :]))
            ya[a:a + SUB, :] = m * inv
            ybt[a:a + SUB, :] = inv

        def y_edge(b, _):
            y_rows(b * (LANES - SUB), SUB)
            return 0
        lax.fori_loop(0, 2, y_edge, 0)

        def back(t, _):
            dst[pl.ds(pl.multiple_of(t * nl, nl), nl), :] = jnp.transpose(yo[pl.ds(t, LANES, stride=SUB), :])
            return 0
        lax.fori_loop(0, SUB, back, 0, unroll=True)
        if s < steps - 1:
            pack_x(s + 1, xs)
            send_x(s + 1)

    for copy in pending:
        copy.wait_send()


def on_device(tracers, air_mass, flux_x, flux_y):
    nt, nlev, nlon, nlat = tracers.shape
    steps, tl = air_mass.shape[:2]
    n_lev, n_x, n_y = lax.axis_size("tracer"), lax.axis_size("gx"), lax.axis_size("gy")
    assert nt == SUB and nlat == LANES and nlev * nlon == LANES and tl == 1 and steps * 4 <= SUB
    rows = nt * nlev * nlon
    V = lambda *shape: pltpu.VMEM(shape, jnp.float32)
    dma = lambda *shape: pltpu.SemaphoreType.DMA(shape)
    H = 3
    out = pl.pallas_call(
        functools.partial(kernel, n_lev, n_x, n_y, steps, tl, nlon),
        out_shape=jax.ShapeDtypeStruct((rows, LANES), jnp.float32),
        in_specs=[pl.BlockSpec(memory_space=pltpu.HBM)] * 4,
        out_specs=pl.BlockSpec(memory_space=pltpu.VMEM),
        scratch_shapes=[
            V(rows, LANES), dma(3 * steps + 1),
            V(steps * n_lev, 3 * nlon, LANES),
            V(SUB, LANES), V(2, SUB, LANES), V(n_lev, SUB, LANES),
            V(steps, 2, n_lev * H * SUB, LANES), V(steps, 2, n_lev * H * SUB, LANES),
            V(steps, 2, (H + 1) * SUB, LANES), V(steps, 2, (H + 1) * SUB, LANES),
            V(rows, LANES), V(rows, LANES), V((LANES + 2 * H) * SUB, LANES), V(LANES * SUB, LANES),
            V(n_lev, nlon + SUB, LANES), V(n_lev, nlon + SUB, LANES), V(n_lev, nlon + SUB, LANES),
            V(n_lev, nlon, LANES), V(n_lev, nlon, LANES),
            V(nlon + 2 * SUB, LANES), V(nlon + SUB, LANES), V(LANES, LANES),
            V(LANES + 2 * SUB, LANES), V(LANES + SUB, LANES), V(LANES + SUB, LANES), V(LANES + SUB, LANES),
            V(LANES, LANES), V(LANES, LANES),
            dma(steps, n_lev), dma(steps, n_lev), dma(2), dma(2), dma(n_lev), dma(n_lev),
            dma(steps, 2), dma(steps, 2), dma(steps, 2), dma(steps, 2),
        ],
        compiler_params=pltpu.CompilerParams(
            collective_id=0, has_side_effects=True, vmem_limit_bytes=56 * 1024 * 1024),
    )(tracers.reshape(rows, LANES), air_mass.reshape(-1, LANES), flux_x.reshape(-1, LANES), flux_y.reshape(-1, LANES))
    return out.reshape(tracers.shape)


def solution(mesh):
    in_specs = (
        P("tracer", None, "gx", "gy"),
        P(None, "tracer", "gx", "gy"),
        P(None, "tracer", "gx", "gy"),
        P(None, "tracer", "gx", "gy"),
    )
    out_specs = P("tracer", None, "gx", "gy")
    return jax.shard_map(
        on_device, mesh=mesh, in_specs=in_specs, out_specs=out_specs, check_vma=False
    )
```

```python
import functools

import jax
import jax.numpy as jnp
from jax import lax
from jax.experimental import pallas as pl
from jax.experimental.pallas import tpu as pltpu
from jax.sharding import PartitionSpec as P

MESH = pl.DeviceIdType.MESH
LANES = 128
SUB = 8


def sweep(q, face, cell, put, begin, end):
    steps, devs, limited, fluxes, rows = {}, {}, {}, {}, {}

    def Q(i):
        if i not in rows:
            rows[i] = q(i)
        return rows[i]

    def D(k):
        if k not in steps:
            steps[k] = Q(k) - Q(k - 1)
        return steps[k]

    def right_of(k):
        if k not in devs:
            raw = 0.5 * D(k) + (1.0 / 12.0) * (D(k - 1) - D(k + 1))
            devs[k] = jnp.minimum(jnp.maximum(raw, jnp.minimum(D(k), 0.0)), jnp.maximum(D(k), 0.0))
        return devs[k]

    def lim(i):
        if i not in limited:
            left, right = D(i) - right_of(i), right_of(i + 1)
            left2, right2 = left + left, right + right
            limited[i] = (
                jnp.minimum(jnp.maximum(left, jnp.minimum(right2, 0.0)), jnp.maximum(right2, 0.0)),
                jnp.minimum(jnp.maximum(right, jnp.minimum(left2, 0.0)), jnp.maximum(left2, 0.0)),
            )
        return limited[i]

    def G(k):
        if k not in fluxes:
            f, near_w, far_w = face(k)
            east = f >= 0.0
            (l0, r0), (l1, r1) = lim(k - 1), lim(k)
            fluxes[k] = (
                f * jnp.where(east, Q(k - 1), Q(k))
                + near_w * jnp.where(east, r0, l1)
                + far_w * jnp.where(east, l0, r1)
            )
        return fluxes[k]

    for i in range(begin, end):
        alpha, beta = cell(i)
        put(i, alpha * Q(i) - beta * (G(i + 1) - G(i)))


def face_weights(f, mass_left, mass_right):
    size = jnp.abs(f)
    c = size / jnp.where(f >= 0.0, mass_left, mass_right)
    rest = 1.0 - c
    part = size * rest
    return part * rest, part * c


def kernel(n_lev, n_x, n_y, steps, tl, nlon, x_hbm, m_ref, fx_ref, fy_ref, o_ref,
           x_ref, in_sem, dyn, eout, ein, edge, hxo, hxi, hyo, hyi, xs, qx, yb, yo,
           cf, cp, cq, ca, cb, mp, fp, mxs, myp, fyp, yp, yq, ya, ybt,
           d_s, d_r, ea_s, ea_r, eb_s, eb_r, hx_s, hx_r, hy_s, hy_r):
    z, gx, gy = lax.axis_index("tracer"), lax.axis_index("gx"), lax.axis_index("gy")
    peers = [lax.rem(z + d, n_lev) for d in range(1, n_lev)]
    left, right = lax.rem(gx + n_x - 1, n_x), lax.rem(gx + 1, n_x)
    south, north = lax.rem(gy + n_y - 1, n_y), lax.rem(gy + 1, n_y)
    H = 3
    nl = n_lev * nlon

    barrier = pltpu.get_barrier_semaphore()
    who = [{"tracer": p} for p in peers] + [{"gx": left}, {"gx": right}, {"gy": south}, {"gy": north}]
    for w in who:
        pl.semaphore_signal(barrier, inc=1, device_id=w, device_id_type=MESH)

    def remote(src, dst, ss, rs, to):
        return pltpu.make_async_remote_copy(src_ref=src, dst_ref=dst, send_sem=ss, recv_sem=rs,
                                            device_id=to, device_id_type=MESH)

    loads = []
    for s in range(steps):
        for f, ref in enumerate((m_ref, fx_ref, fy_ref)):
            loads.append(pltpu.make_async_copy(
                ref.at[pl.ds(s * nlon, nlon)], dyn.at[s * n_lev + z, pl.ds(f * nlon, nlon)], in_sem.at[len(loads)]))
            loads[-1].start()
    load_x = pltpu.make_async_copy(x_hbm, x_ref, in_sem.at[len(loads)])
    load_x.start()

    def pack_x(s, src):
        def body(lev, _):
            for c in range(H):
                to = pl.ds(pl.multiple_of((lev * H + c) * SUB, SUB), SUB)
                hxo[s, 0, to, :] = src[pl.ds(lev * nlon + c, SUB, stride=nl), :]
                hxo[s, 1, to, :] = src[pl.ds(lev * nlon + nlon - H + c, SUB, stride=nl), :]
            return 0
        lax.fori_loop(0, n_lev, body, 0, unroll=True)

    for copy in loads:
        copy.wait()
    for s in range(steps):
        own = s * n_lev + z
        eout[s * 4:s * 4 + 1, :] = dyn[own, nlon - 1:nlon, :]
        eout[s * 4 + 1:s * 4 + 2, :] = dyn[own, 0:1, :]
        eout[s * 4 + 2:s * 4 + 3, :] = dyn[own, nlon:nlon + 1, :]
        eout[s * 4 + 3:s * 4 + 4, :] = dyn[own, nlon:nlon + 1, :]
    mp[0:SUB, :] = jnp.ones((SUB, LANES), jnp.float32)
    fp[nlon:nlon + SUB, :] = jnp.zeros((SUB, LANES), jnp.float32)
    load_x.wait()
    pack_x(0, x_ref)
    pl.semaphore_wait(barrier, len(who))

    pending = []

    def go(copy):
        copy.start()
        pending.append(copy)

    go(remote(eout, ein.at[1], ea_s.at[0], ea_r.at[1], {"gx": left}))
    go(remote(eout, ein.at[0], ea_s.at[1], ea_r.at[0], {"gx": right}))

    def send_dyn(s):
        for d, p in enumerate(peers):
            go(remote(dyn.at[s * n_lev + z], dyn.at[s * n_lev + z], d_s.at[s, d], d_r.at[s, z], {"tracer": p}))

    def send_x(s):
        go(remote(hxo.at[s, 0], hxi.at[s, 1], hx_s.at[s, 0], hx_r.at[s, 1], {"gx": left}))
        go(remote(hxo.at[s, 1], hxi.at[s, 0], hx_s.at[s, 1], hx_r.at[s, 0], {"gx": right}))

    send_x(0)
    send_dyn(0)

    def share_edges():
        for side in range(2):
            remote(eout, ein.at[side], ea_s.at[side], ea_r.at[side], {"gx": left}).wait_recv()
        for s in range(steps):
            edge[z, s * 4:s * 4 + 1, :] = ein[0, s * 4:s * 4 + 1, :]
            edge[z, s * 4 + 1:s * 4 + 4, :] = ein[1, s * 4 + 1:s * 4 + 4, :]
        for d, p in enumerate(peers):
            go(remote(edge.at[z], edge.at[z], eb_s.at[d], eb_r.at[z], {"tracer": p}))

    for s in range(steps):
        src = x_ref if s == 0 else xs
        dst = xs if s < steps - 1 else o_ref

        def x_inner(j, _):
            lev = lax.rem(z + j, n_lev)
            slot = s * n_lev + lev

            def here():
                remote(dyn.at[slot], dyn.at[slot], d_s.at[s, 0], d_r.at[s, lev], {"tracer": z}).wait_recv()
            if s > 0:
                pl.when(j > 0)(here)
            elif not isinstance(j, int):
                here()

            m = dyn[slot, 0:nlon, :]
            mp[SUB:SUB + nlon, :] = m
            fp[0:nlon, :] = dyn[slot, nlon:2 * nlon, :]
            f = fp[0:nlon, :]
            pw, qw = face_weights(f, mp[SUB - 1:SUB - 1 + nlon, :], m)
            cf[lev, 0:nlon, :] = f
            cp[lev, 0:nlon, :] = pw
            cq[lev, 0:nlon, :] = qw
            mx = m - (fp[1:nlon + 1, :] - f)
            inv = 1.0 / mx
            ca[lev] = m * inv
            cb[lev] = inv
            mxs[pl.ds(pl.multiple_of(lev * nlon, nlon), nlon), :] = mx
            base = lev * nlon
            sweep(
                lambda i: src[pl.ds(base + i, SUB, stride=nl), :],
                lambda k: (cf[lev, k:k + 1, :], cp[lev, k:k + 1, :], cq[lev, k:k + 1, :]),
                lambda i: (ca[lev, i:i + 1, :], cb[lev, i:i + 1, :]),
                functools.partial(put_x, base), H, nlon - H)
            return 0

        def put_x(base, i, v):
            qx[pl.ds(base + i, SUB, stride=nl), :] = v

        if s == 0:
            x_inner(0, 0)
            share_edges()
            lax.fori_loop(1, n_lev, x_inner, 0)

            def edge_here(j, _):
                lev = lax.rem(z + j, n_lev)
                remote(edge.at[lev], edge.at[lev], eb_s.at[0], eb_r.at[lev], {"tracer": z}).wait_recv()
                return 0
            lax.fori_loop(1, n_lev, edge_here, 0)
            for later in range(1, steps):
                send_dyn(later)
        else:
            lax.fori_loop(0, n_lev, x_inner, 0)
        for side in range(2):
            remote(hxo.at[s, 0], hxi.at[s, side], hx_s.at[s, side], hx_r.at[s, side], {"gx": left}).wait_recv()

        def x_edge(lev, _):
            base = lev * nlon
            slot = s * n_lev + lev
            first = slice(nlon, nlon + 1)
            m_w = edge[lev, s * 4:s * 4 + 1, :]
            m_e = edge[lev, s * 4 + 1:s * 4 + 2, :]
            f_e = edge[lev, s * 4 + 2:s * 4 + 3, :]
            f_w = dyn[slot, first, :]
            pw, qw = face_weights(f_w, m_w, dyn[slot, 0:1, :])
            cp[lev, 0:1, :] = pw
            cq[lev, 0:1, :] = qw
            m_last = dyn[slot, nlon - 1:nlon, :]
            pw, qw = face_weights(f_e, m_last, m_e)
            cf[lev, first, :] = f_e
            cp[lev, first, :] = pw
            cq[lev, first, :] = qw
            mx = m_last - (f_e - dyn[slot, 2 * nlon - 1:2 * nlon, :])
            inv = 1.0 / mx
            ca[lev, nlon - 1:nlon, :] = m_last * inv
            cb[lev, nlon - 1:nlon, :] = inv
            mxs[pl.ds(base + nlon - 1, 1), :] = mx

            def q(i):
                if i < 0:
                    return hxi[s, 0, pl.ds(pl.multiple_of((lev * H + i + H) * SUB, SUB), SUB), :]
                if i >= nlon:
                    return hxi[s, 1, pl.ds(pl.multiple_of((lev * H + i - nlon) * SUB, SUB), SUB), :]
                return src[pl.ds(base + i, SUB, stride=nl), :]

            for a, b in ((0, H), (nlon - H, nlon)):
                sweep(
                    q,
                    lambda k: (cf[lev, k:k + 1, :], cp[lev, k:k + 1, :], cq[lev, k:k + 1, :]),
                    lambda i: (ca[lev, i:i + 1, :], cb[lev, i:i + 1, :]),
                    functools.partial(put_x, base), a, b)
            return 0

        lax.fori_loop(0, n_lev, x_edge, 0, unroll=True)

        off = H * SUB

        mt = jnp.transpose(mxs[...])
        ft = jnp.transpose(jnp.concatenate(
            [dyn[s * n_lev + lev, 2 * nlon:3 * nlon, :] for lev in range(n_lev)], axis=0))
        myp[SUB:SUB + LANES, :] = mt
        fyp[0:LANES, :] = ft

        def turn(t, _):
            yb[pl.ds(off + t, LANES, stride=SUB), :] = jnp.transpose(qx[t * nl:(t + 1) * nl, :])
        for t in range(SUB):
            turn(t, 0)
        extra = jnp.concatenate([mt[0:1], mt[LANES - 1:LANES], ft[0:1], ft[0:1], ft[0:1], ft[0:1], ft[0:1], ft[0:1]], axis=0)
        for side in range(2):
            hyo[s, side, H * SUB:(H + 1) * SUB, :] = extra
        hyo[s, 0, 0:H * SUB, :] = yb[off:off + H * SUB, :]
        hyo[s, 1, 0:H * SUB, :] = yb[off + (LANES - H) * SUB:off + LANES * SUB, :]
        go(remote(hyo.at[s, 0], hyi.at[s, 1], hy_s.at[s, 0], hy_r.at[s, 1], {"gy": south}))
        go(remote(hyo.at[s, 1], hyi.at[s, 0], hy_s.at[s, 1], hy_r.at[s, 0], {"gy": north}))

        f = fyp[SUB:LANES, :]
        pw, qw = face_weights(f, myp[2 * SUB - 1:SUB + LANES - 1, :], myp[2 * SUB:SUB + LANES, :])
        yp[SUB:LANES, :] = pw
        yq[SUB:LANES, :] = qw
        m = myp[SUB:LANES, :]
        inv = 1.0 / (m - (fyp[1:LANES - SUB + 1, :] - fyp[0:LANES - SUB, :]))
        ya[0:LANES - SUB, :] = m * inv
        ybt[0:LANES - SUB, :] = inv

        def y_rows(first, count):
            sweep(
                lambda i: yb[pl.ds(pl.multiple_of(off + (first + i) * SUB, SUB), SUB), :],
                lambda k: (fyp[pl.ds(first + k, 1), :], yp[pl.ds(first + k, 1), :], yq[pl.ds(first + k, 1), :]),
                lambda i: (ya[pl.ds(first + i, 1), :], ybt[pl.ds(first + i, 1), :]),
                put_y(first), 0, count)

        def put_y(first):
            def put(i, v):
                yo[pl.ds(pl.multiple_of((first + i) * SUB, SUB), SUB), :] = v
            return put

        def y_inner(b, _):
            y_rows(SUB + b * 16, 16)
            return 0
        lax.fori_loop(0, (LANES - 2 * SUB) // 16, y_inner, 0)

        for side in range(2):
            remote(hyo.at[s, 0], hyi.at[s, side], hy_s.at[s, side], hy_r.at[s, side], {"gy": south}).wait_recv()
        at_south, at_north = gy == 0, gy == n_y - 1
        yb[0:H * SUB, :] = jnp.where(at_south, 0.0, hyi[s, 0, 0:H * SUB, :])
        yb[off + LANES * SUB:off + (LANES + H) * SUB, :] = jnp.where(at_north, 0.0, hyi[s, 1, 0:H * SUB, :])
        e = H * SUB
        myp[0:SUB, :] = jnp.broadcast_to(jnp.where(at_south, 1.0, hyi[s, 0, e + 1:e + 2, :]), (SUB, LANES))
        myp[SUB + LANES:2 * SUB + LANES, :] = jnp.broadcast_to(
            jnp.where(at_north, 1.0, hyi[s, 1, e:e + 1, :]), (SUB, LANES))
        fyp[LANES:LANES + SUB, :] = jnp.broadcast_to(
            jnp.where(at_north, 0.0, hyi[s, 1, e + 2:e + 3, :]), (SUB, LANES))
        fyp[0:1, :] = jnp.where(at_south, 0.0, fyp[0:1, :])
        for a in (0, LANES):
            f = fyp[a:a + SUB, :]
            pw, qw = face_weights(f, myp[a + SUB - 1:a + 2 * SUB - 1, :], myp[a + SUB:a + 2 * SUB, :])
            yp[a:a + SUB, :] = pw
            yq[a:a + SUB, :] = qw
        for a in (0, LANES - SUB):
            m = myp[a + SUB:a + 2 * SUB, :]
            inv = 1.0 / (m - (fyp[a + 1:a + SUB + 1, :] - fyp[a:a + SUB, :]))
            ya[a:a + SUB, :] = m * inv
            ybt[a:a + SUB, :] = inv

        def y_edge(b, _):
            y_rows(b * (LANES - SUB), SUB)
            return 0
        lax.fori_loop(0, 2, y_edge, 0, unroll=True)

        def back(t, _):
            dst[t * nl:(t + 1) * nl, :] = jnp.transpose(yo[pl.ds(t, LANES, stride=SUB), :])
        for t in range(SUB):
            back(t, 0)
        if s < steps - 1:
            pack_x(s + 1, xs)
            send_x(s + 1)

    for copy in pending:
        copy.wait_send()


def on_device(tracers, air_mass, flux_x, flux_y):
    nt, nlev, nlon, nlat = tracers.shape
    steps, tl = air_mass.shape[:2]
    n_lev, n_x, n_y = lax.axis_size("tracer"), lax.axis_size("gx"), lax.axis_size("gy")
    assert nt == SUB and nlat == LANES and nlev * nlon == LANES and tl == 1 and steps * 4 <= SUB
    rows = nt * nlev * nlon
    V = lambda *shape: pltpu.VMEM(shape, jnp.float32)
    dma = lambda *shape: pltpu.SemaphoreType.DMA(shape)
    H = 3
    out = pl.pallas_call(
        functools.partial(kernel, n_lev, n_x, n_y, steps, tl, nlon),
        out_shape=jax.ShapeDtypeStruct((rows, LANES), jnp.float32),
        in_specs=[pl.BlockSpec(memory_space=pltpu.HBM)] * 4,
        out_specs=pl.BlockSpec(memory_space=pltpu.VMEM),
        scratch_shapes=[
            V(rows, LANES), dma(3 * steps + 1),
            V(steps * n_lev, 3 * nlon, LANES),
            V(SUB, LANES), V(2, SUB, LANES), V(n_lev, SUB, LANES),
            V(steps, 2, n_lev * H * SUB, LANES), V(steps, 2, n_lev * H * SUB, LANES),
            V(steps, 2, (H + 1) * SUB, LANES), V(steps, 2, (H + 1) * SUB, LANES),
            V(rows, LANES), V(rows, LANES), V((LANES + 2 * H) * SUB, LANES), V(LANES * SUB, LANES),
            V(n_lev, nlon + SUB, LANES), V(n_lev, nlon + SUB, LANES), V(n_lev, nlon + SUB, LANES),
            V(n_lev, nlon, LANES), V(n_lev, nlon, LANES),
            V(nlon + 2 * SUB, LANES), V(nlon + SUB, LANES), V(LANES, LANES),
            V(LANES + 2 * SUB, LANES), V(LANES + SUB, LANES), V(LANES + SUB, LANES), V(LANES + SUB, LANES),
            V(LANES, LANES), V(LANES, LANES),
            dma(steps, n_lev), dma(steps, n_lev), dma(2), dma(2), dma(n_lev), dma(n_lev),
            dma(steps, 2), dma(steps, 2), dma(steps, 2), dma(steps, 2),
        ],
        compiler_params=pltpu.CompilerParams(
            collective_id=0, has_side_effects=True, vmem_limit_bytes=56 * 1024 * 1024),
    )(tracers.reshape(rows, LANES), air_mass.reshape(-1, LANES), flux_x.reshape(-1, LANES), flux_y.reshape(-1, LANES))
    return out.reshape(tracers.shape)


def solution(mesh):
    in_specs = (
        P("tracer", None, "gx", "gy"),
        P(None, "tracer", "gx", "gy"),
        P(None, "tracer", "gx", "gy"),
        P(None, "tracer", "gx", "gy"),
    )
    out_specs = P("tracer", None, "gx", "gy")
    return jax.shard_map(
        on_device, mesh=mesh, in_specs=in_specs, out_specs=out_specs, check_vma=False
    )
```

```python
import functools

import jax
import jax.numpy as jnp
from jax import lax
from jax.experimental import pallas as pl
from jax.experimental.pallas import tpu as pltpu
from jax.sharding import PartitionSpec as P

MESH = pl.DeviceIdType.MESH
LANES = 128
SUB = 8


def sweep(q, face, cell, put, begin, end):
    steps, devs, limited, fluxes, rows = {}, {}, {}, {}, {}

    def Q(i):
        if i not in rows:
            rows[i] = q(i)
        return rows[i]

    def D(k):
        if k not in steps:
            steps[k] = Q(k) - Q(k - 1)
        return steps[k]

    def right_of(k):
        if k not in devs:
            raw = 0.5 * D(k) + (1.0 / 12.0) * (D(k - 1) - D(k + 1))
            devs[k] = jnp.minimum(jnp.maximum(raw, jnp.minimum(D(k), 0.0)), jnp.maximum(D(k), 0.0))
        return devs[k]

    def lim(i):
        if i not in limited:
            left, right = D(i) - right_of(i), right_of(i + 1)
            left2, right2 = left + left, right + right
            limited[i] = (
                jnp.minimum(jnp.maximum(left, jnp.minimum(right2, 0.0)), jnp.maximum(right2, 0.0)),
                jnp.minimum(jnp.maximum(right, jnp.minimum(left2, 0.0)), jnp.maximum(left2, 0.0)),
            )
        return limited[i]

    def G(k):
        if k not in fluxes:
            f, near_w, far_w = face(k)
            east = f >= 0.0
            (l0, r0), (l1, r1) = lim(k - 1), lim(k)
            fluxes[k] = (
                f * jnp.where(east, Q(k - 1), Q(k))
                + near_w * jnp.where(east, r0, l1)
                + far_w * jnp.where(east, l0, r1)
            )
        return fluxes[k]

    for i in range(begin, end):
        alpha, beta = cell(i)
        put(i, alpha * Q(i) - beta * (G(i + 1) - G(i)))


def face_weights(f, mass_left, mass_right):
    size = jnp.abs(f)
    c = size / jnp.where(f >= 0.0, mass_left, mass_right)
    rest = 1.0 - c
    part = size * rest
    return part * rest, part * c


def kernel(n_lev, n_x, n_y, steps, tl, nlon, x_hbm, m_ref, fx_ref, fy_ref, o_ref,
           x_ref, in_sem, dyn, eout, ein, edge, hxo, hxi, hyo, hyi, xs, qx, yb, yo,
           cf, cp, cq, ca, cb, mp, fp, mxs, myp, fyp, yp, yq, ya, ybt,
           d_s, d_r, ea_s, ea_r, eb_s, eb_r, hx_s, hx_r, hy_s, hy_r):
    z, gx, gy = lax.axis_index("tracer"), lax.axis_index("gx"), lax.axis_index("gy")
    peers = [lax.rem(z + d, n_lev) for d in range(1, n_lev)]
    left, right = lax.rem(gx + n_x - 1, n_x), lax.rem(gx + 1, n_x)
    south, north = lax.rem(gy + n_y - 1, n_y), lax.rem(gy + 1, n_y)
    H = 3
    nl = n_lev * nlon

    barrier = pltpu.get_barrier_semaphore()
    who = [{"tracer": p} for p in peers] + [{"gx": left}, {"gx": right}, {"gy": south}, {"gy": north}]
    for w in who:
        pl.semaphore_signal(barrier, inc=1, device_id=w, device_id_type=MESH)

    def remote(src, dst, ss, rs, to):
        return pltpu.make_async_remote_copy(src_ref=src, dst_ref=dst, send_sem=ss, recv_sem=rs,
                                            device_id=to, device_id_type=MESH)

    loads = []
    for s in range(steps):
        for f, ref in enumerate((m_ref, fx_ref, fy_ref)):
            loads.append(pltpu.make_async_copy(
                ref.at[pl.ds(s * nlon, nlon)], dyn.at[s * n_lev + z, pl.ds(f * nlon, nlon)], in_sem.at[len(loads)]))
            loads[-1].start()
    load_x = pltpu.make_async_copy(x_hbm, x_ref, in_sem.at[len(loads)])
    load_x.start()

    def pack_x(s, src):
        def body(lev, _):
            for c in range(H):
                to = pl.ds(pl.multiple_of((lev * H + c) * SUB, SUB), SUB)
                hxo[s, 0, to, :] = src[pl.ds(lev * nlon + c, SUB, stride=nl), :]
                hxo[s, 1, to, :] = src[pl.ds(lev * nlon + nlon - H + c, SUB, stride=nl), :]
            return 0
        lax.fori_loop(0, n_lev, body, 0, unroll=True)

    for copy in loads:
        copy.wait()
    for s in range(steps):
        own = s * n_lev + z
        eout[s * 4:s * 4 + 1, :] = dyn[own, nlon - 1:nlon, :]
        eout[s * 4 + 1:s * 4 + 2, :] = dyn[own, 0:1, :]
        eout[s * 4 + 2:s * 4 + 3, :] = dyn[own, nlon:nlon + 1, :]
        eout[s * 4 + 3:s * 4 + 4, :] = dyn[own, nlon:nlon + 1, :]
    mp[0:SUB, :] = jnp.ones((SUB, LANES), jnp.float32)
    fp[nlon:nlon + SUB, :] = jnp.zeros((SUB, LANES), jnp.float32)
    load_x.wait()
    pack_x(0, x_ref)
    pl.semaphore_wait(barrier, len(who))

    pending = []

    def go(copy):
        copy.start()
        pending.append(copy)

    go(remote(eout, ein.at[1], ea_s.at[0], ea_r.at[1], {"gx": left}))
    go(remote(eout, ein.at[0], ea_s.at[1], ea_r.at[0], {"gx": right}))

    def send_dyn(s):
        for d, p in enumerate(peers):
            go(remote(dyn.at[s * n_lev + z], dyn.at[s * n_lev + z], d_s.at[s, d], d_r.at[s, z], {"tracer": p}))

    def send_x(s):
        go(remote(hxo.at[s, 0], hxi.at[s, 1], hx_s.at[s, 0], hx_r.at[s, 1], {"gx": left}))
        go(remote(hxo.at[s, 1], hxi.at[s, 0], hx_s.at[s, 1], hx_r.at[s, 0], {"gx": right}))

    send_x(0)
    send_dyn(0)

    def share_edges():
        for side in range(2):
            remote(eout, ein.at[side], ea_s.at[side], ea_r.at[side], {"gx": left}).wait_recv()
        for s in range(steps):
            edge[z, s * 4:s * 4 + 1, :] = ein[0, s * 4:s * 4 + 1, :]
            edge[z, s * 4 + 1:s * 4 + 4, :] = ein[1, s * 4 + 1:s * 4 + 4, :]
        for d, p in enumerate(peers):
            go(remote(edge.at[z], edge.at[z], eb_s.at[d], eb_r.at[z], {"tracer": p}))

    for s in range(steps):
        src = x_ref if s == 0 else xs
        dst = xs if s < steps - 1 else o_ref

        def x_inner(j, _):
            lev = lax.rem(z + j, n_lev)
            slot = s * n_lev + lev

            def here():
                remote(dyn.at[slot], dyn.at[slot], d_s.at[s, 0], d_r.at[s, lev], {"tracer": z}).wait_recv()
            if s > 0:
                pl.when(j > 0)(here)
            elif not isinstance(j, int):
                here()

            m = dyn[slot, 0:nlon, :]
            mp[SUB:SUB + nlon, :] = m
            fp[0:nlon, :] = dyn[slot, nlon:2 * nlon, :]
            f = fp[0:nlon, :]
            pw, qw = face_weights(f, mp[SUB - 1:SUB - 1 + nlon, :], m)
            cf[lev, 0:nlon, :] = f
            cp[lev, 0:nlon, :] = pw
            cq[lev, 0:nlon, :] = qw
            mx = m - (fp[1:nlon + 1, :] - f)
            inv = 1.0 / mx
            ca[lev] = m * inv
            cb[lev] = inv
            mxs[pl.ds(pl.multiple_of(lev * nlon, nlon), nlon), :] = mx
            base = lev * nlon
            sweep(
                lambda i: src[pl.ds(base + i, SUB, stride=nl), :],
                lambda k: (cf[lev, k:k + 1, :], cp[lev, k:k + 1, :], cq[lev, k:k + 1, :]),
                lambda i: (ca[lev, i:i + 1, :], cb[lev, i:i + 1, :]),
                functools.partial(put_x, base), H, nlon - H)
            return 0

        def put_x(base, i, v):
            qx[pl.ds(base + i, SUB, stride=nl), :] = v

        if s == 0:
            x_inner(0, 0)
            share_edges()
            lax.fori_loop(1, n_lev, x_inner, 0)

            def edge_here(j, _):
                lev = lax.rem(z + j, n_lev)
                remote(edge.at[lev], edge.at[lev], eb_s.at[0], eb_r.at[lev], {"tracer": z}).wait_recv()
                return 0
            lax.fori_loop(1, n_lev, edge_here, 0)
        else:
            lax.fori_loop(0, n_lev, x_inner, 0)
        for side in range(2):
            remote(hxo.at[s, 0], hxi.at[s, side], hx_s.at[s, side], hx_r.at[s, side], {"gx": left}).wait_recv()

        for later in range(1, steps) if s == 0 else ():
            send_dyn(later)
        def x_edge(lev, _):
            base = lev * nlon
            slot = s * n_lev + lev
            first = slice(nlon, nlon + 1)
            m_w = edge[lev, s * 4:s * 4 + 1, :]
            m_e = edge[lev, s * 4 + 1:s * 4 + 2, :]
            f_e = edge[lev, s * 4 + 2:s * 4 + 3, :]
            f_w = dyn[slot, first, :]
            pw, qw = face_weights(f_w, m_w, dyn[slot, 0:1, :])
            cp[lev, 0:1, :] = pw
            cq[lev, 0:1, :] = qw
            m_last = dyn[slot, nlon - 1:nlon, :]
            pw, qw = face_weights(f_e, m_last, m_e)
            cf[lev, first, :] = f_e
            cp[lev, first, :] = pw
            cq[lev, first, :] = qw
            mx = m_last - (f_e - dyn[slot, 2 * nlon - 1:2 * nlon, :])
            inv = 1.0 / mx
            ca[lev, nlon - 1:nlon, :] = m_last * inv
            cb[lev, nlon - 1:nlon, :] = inv
            mxs[pl.ds(base + nlon - 1, 1), :] = mx

            def q(i):
                if i < 0:
                    return hxi[s, 0, pl.ds(pl.multiple_of((lev * H + i + H) * SUB, SUB), SUB), :]
                if i >= nlon:
                    return hxi[s, 1, pl.ds(pl.multiple_of((lev * H + i - nlon) * SUB, SUB), SUB), :]
                return src[pl.ds(base + i, SUB, stride=nl), :]

            for a, b in ((0, H), (nlon - H, nlon)):
                sweep(
                    q,
                    lambda k: (cf[lev, k:k + 1, :], cp[lev, k:k + 1, :], cq[lev, k:k + 1, :]),
                    lambda i: (ca[lev, i:i + 1, :], cb[lev, i:i + 1, :]),
                    functools.partial(put_x, base), a, b)
            return 0

        lax.fori_loop(0, n_lev, x_edge, 0, unroll=True)

        off = H * SUB

        mt = jnp.transpose(mxs[...])
        ft = jnp.transpose(jnp.concatenate(
            [dyn[s * n_lev + lev, 2 * nlon:3 * nlon, :] for lev in range(n_lev)], axis=0))
        myp[SUB:SUB + LANES, :] = mt
        fyp[0:LANES, :] = ft

        def turn(t, _):
            yb[pl.ds(off + t, LANES, stride=SUB), :] = jnp.transpose(qx[t * nl:(t + 1) * nl, :])
        for t in range(SUB):
            turn(t, 0)
        extra = jnp.concatenate([mt[0:1], mt[LANES - 1:LANES], ft[0:1], ft[0:1], ft[0:1], ft[0:1], ft[0:1], ft[0:1]], axis=0)
        for side in range(2):
            hyo[s, side, H * SUB:(H + 1) * SUB, :] = extra
        hyo[s, 0, 0:H * SUB, :] = yb[off:off + H * SUB, :]
        hyo[s, 1, 0:H * SUB, :] = yb[off + (LANES - H) * SUB:off + LANES * SUB, :]
        go(remote(hyo.at[s, 0], hyi.at[s, 1], hy_s.at[s, 0], hy_r.at[s, 1], {"gy": south}))
        go(remote(hyo.at[s, 1], hyi.at[s, 0], hy_s.at[s, 1], hy_r.at[s, 0], {"gy": north}))

        f = fyp[SUB:LANES, :]
        pw, qw = face_weights(f, myp[2 * SUB - 1:SUB + LANES - 1, :], myp[2 * SUB:SUB + LANES, :])
        yp[SUB:LANES, :] = pw
        yq[SUB:LANES, :] = qw
        m = myp[SUB:LANES, :]
        inv = 1.0 / (m - (fyp[1:LANES - SUB + 1, :] - fyp[0:LANES - SUB, :]))
        ya[0:LANES - SUB, :] = m * inv
        ybt[0:LANES - SUB, :] = inv

        def y_rows(first, count):
            sweep(
                lambda i: yb[pl.ds(pl.multiple_of(off + (first + i) * SUB, SUB), SUB), :],
                lambda k: (fyp[pl.ds(first + k, 1), :], yp[pl.ds(first + k, 1), :], yq[pl.ds(first + k, 1), :]),
                lambda i: (ya[pl.ds(first + i, 1), :], ybt[pl.ds(first + i, 1), :]),
                put_y(first), 0, count)

        def put_y(first):
            def put(i, v):
                yo[pl.ds(pl.multiple_of((first + i) * SUB, SUB), SUB), :] = v
            return put

        def y_inner(b, _):
            y_rows(SUB + b * 28, 28)
            return 0
        lax.fori_loop(0, (LANES - 2 * SUB) // 28, y_inner, 0)

        for side in range(2):
            remote(hyo.at[s, 0], hyi.at[s, side], hy_s.at[s, side], hy_r.at[s, side], {"gy": south}).wait_recv()
        at_south, at_north = gy == 0, gy == n_y - 1
        yb[0:H * SUB, :] = jnp.where(at_south, 0.0, hyi[s, 0, 0:H * SUB, :])
        yb[off + LANES * SUB:off + (LANES + H) * SUB, :] = jnp.where(at_north, 0.0, hyi[s, 1, 0:H * SUB, :])
        e = H * SUB
        myp[0:SUB, :] = jnp.broadcast_to(jnp.where(at_south, 1.0, hyi[s, 0, e + 1:e + 2, :]), (SUB, LANES))
        myp[SUB + LANES:2 * SUB + LANES, :] = jnp.broadcast_to(
            jnp.where(at_north, 1.0, hyi[s, 1, e:e + 1, :]), (SUB, LANES))
        fyp[LANES:LANES + SUB, :] = jnp.broadcast_to(
            jnp.where(at_north, 0.0, hyi[s, 1, e + 2:e + 3, :]), (SUB, LANES))
        fyp[0:1, :] = jnp.where(at_south, 0.0, fyp[0:1, :])
        for a in (0, LANES):
            f = fyp[a:a + SUB, :]
            pw, qw = face_weights(f, myp[a + SUB - 1:a + 2 * SUB - 1, :], myp[a + SUB:a + 2 * SUB, :])
            yp[a:a + SUB, :] = pw
            yq[a:a + SUB, :] = qw
        for a in (0, LANES - SUB):
            m = myp[a + SUB:a + 2 * SUB, :]
            inv = 1.0 / (m - (fyp[a + 1:a + SUB + 1, :] - fyp[a:a + SUB, :]))
            ya[a:a + SUB, :] = m * inv
            ybt[a:a + SUB, :] = inv

        def y_edge(b, _):
            y_rows(b * (LANES - SUB), SUB)
            return 0
        lax.fori_loop(0, 2, y_edge, 0, unroll=True)

        def back(t, _):
            dst[t * nl:(t + 1) * nl, :] = jnp.transpose(yo[pl.ds(t, LANES, stride=SUB), :])
        for t in range(SUB):
            back(t, 0)
        if s < steps - 1:
            pack_x(s + 1, xs)
            send_x(s + 1)

    for copy in pending:
        copy.wait_send()


def on_device(tracers, air_mass, flux_x, flux_y):
    nt, nlev, nlon, nlat = tracers.shape
    steps, tl = air_mass.shape[:2]
    n_lev, n_x, n_y = lax.axis_size("tracer"), lax.axis_size("gx"), lax.axis_size("gy")
    assert nt == SUB and nlat == LANES and nlev * nlon == LANES and tl == 1 and steps * 4 <= SUB
    rows = nt * nlev * nlon
    V = lambda *shape: pltpu.VMEM(shape, jnp.float32)
    dma = lambda *shape: pltpu.SemaphoreType.DMA(shape)
    H = 3
    out = pl.pallas_call(
        functools.partial(kernel, n_lev, n_x, n_y, steps, tl, nlon),
        out_shape=jax.ShapeDtypeStruct((rows, LANES), jnp.float32),
        in_specs=[pl.BlockSpec(memory_space=pltpu.HBM)] * 4,
        out_specs=pl.BlockSpec(memory_space=pltpu.VMEM),
        scratch_shapes=[
            V(rows, LANES), dma(3 * steps + 1),
            V(steps * n_lev, 3 * nlon, LANES),
            V(SUB, LANES), V(2, SUB, LANES), V(n_lev, SUB, LANES),
            V(steps, 2, n_lev * H * SUB, LANES), V(steps, 2, n_lev * H * SUB, LANES),
            V(steps, 2, (H + 1) * SUB, LANES), V(steps, 2, (H + 1) * SUB, LANES),
            V(rows, LANES), V(rows, LANES), V((LANES + 2 * H) * SUB, LANES), V(LANES * SUB, LANES),
            V(n_lev, nlon + SUB, LANES), V(n_lev, nlon + SUB, LANES), V(n_lev, nlon + SUB, LANES),
            V(n_lev, nlon, LANES), V(n_lev, nlon, LANES),
            V(nlon + 2 * SUB, LANES), V(nlon + SUB, LANES), V(LANES, LANES),
            V(LANES + 2 * SUB, LANES), V(LANES + SUB, LANES), V(LANES + SUB, LANES), V(LANES + SUB, LANES),
            V(LANES, LANES), V(LANES, LANES),
            dma(steps, n_lev), dma(steps, n_lev), dma(2), dma(2), dma(n_lev), dma(n_lev),
            dma(steps, 2), dma(steps, 2), dma(steps, 2), dma(steps, 2),
        ],
        compiler_params=pltpu.CompilerParams(
            collective_id=0, has_side_effects=True, vmem_limit_bytes=56 * 1024 * 1024),
    )(tracers.reshape(rows, LANES), air_mass.reshape(-1, LANES), flux_x.reshape(-1, LANES), flux_y.reshape(-1, LANES))
    return out.reshape(tracers.shape)


def solution(mesh):
    in_specs = (
        P("tracer", None, "gx", "gy"),
        P(None, "tracer", "gx", "gy"),
        P(None, "tracer", "gx", "gy"),
        P(None, "tracer", "gx", "gy"),
    )
    out_specs = P("tracer", None, "gx", "gy")
    return jax.shard_map(
        on_device, mesh=mesh, in_specs=in_specs, out_specs=out_specs, check_vma=False
    )
```

```python
import functools

import jax
import jax.numpy as jnp
from jax import lax
from jax.experimental import pallas as pl
from jax.experimental.pallas import tpu as pltpu
from jax.sharding import PartitionSpec as P

MESH = pl.DeviceIdType.MESH
LANES = 128
SUB = 8


def sweep(q, face, cell, put, begin, end):
    steps, devs, limited, fluxes, rows = {}, {}, {}, {}, {}

    def Q(i):
        if i not in rows:
            rows[i] = q(i)
        return rows[i]

    def D(k):
        if k not in steps:
            steps[k] = Q(k) - Q(k - 1)
        return steps[k]

    def right_of(k):
        if k not in devs:
            raw = 0.5 * D(k) + (1.0 / 12.0) * (D(k - 1) - D(k + 1))
            devs[k] = jnp.minimum(jnp.maximum(raw, jnp.minimum(D(k), 0.0)), jnp.maximum(D(k), 0.0))
        return devs[k]

    def lim(i):
        if i not in limited:
            left, right = D(i) - right_of(i), right_of(i + 1)
            left2, right2 = left + left, right + right
            limited[i] = (
                jnp.minimum(jnp.maximum(left, jnp.minimum(right2, 0.0)), jnp.maximum(right2, 0.0)),
                jnp.minimum(jnp.maximum(right, jnp.minimum(left2, 0.0)), jnp.maximum(left2, 0.0)),
            )
        return limited[i]

    def G(k):
        if k not in fluxes:
            f, near_w, far_w = face(k)
            east = f >= 0.0
            (l0, r0), (l1, r1) = lim(k - 1), lim(k)
            fluxes[k] = (
                f * jnp.where(east, Q(k - 1), Q(k))
                + near_w * jnp.where(east, r0, l1)
                + far_w * jnp.where(east, l0, r1)
            )
        return fluxes[k]

    for i in range(begin, end):
        alpha, beta = cell(i)
        put(i, alpha * Q(i) - beta * (G(i + 1) - G(i)))


def face_weights(f, mass_left, mass_right):
    size = jnp.abs(f)
    c = size / jnp.where(f >= 0.0, mass_left, mass_right)
    rest = 1.0 - c
    part = size * rest
    return part * rest, part * c


def kernel(n_lev, n_x, n_y, steps, tl, nlon, x_hbm, m_ref, fx_ref, fy_ref, o_ref,
           x_ref, in_sem, dyn, eout, ein, edge, hxo, hxi, hyo, hyi, xs, qx, yb, yo,
           cf, cp, cq, ca, cb, mp, fp, mxs, myp, fyp, yp, yq, ya, ybt,
           d_s, d_r, ea_s, ea_r, eb_s, eb_r, hx_s, hx_r, hy_s, hy_r):
    z, gx, gy = lax.axis_index("tracer"), lax.axis_index("gx"), lax.axis_index("gy")
    peers = [lax.rem(z + n_lev - d, n_lev) for d in range(1, n_lev)]
    left, right = lax.rem(gx + n_x - 1, n_x), lax.rem(gx + 1, n_x)
    south, north = lax.rem(gy + n_y - 1, n_y), lax.rem(gy + 1, n_y)
    H = 3
    nl = n_lev * nlon

    barrier = pltpu.get_barrier_semaphore()
    who = [{"tracer": p} for p in peers] + [{"gx": left}, {"gx": right}, {"gy": south}, {"gy": north}]
    for w in who:
        pl.semaphore_signal(barrier, inc=1, device_id=w, device_id_type=MESH)

    def remote(src, dst, ss, rs, to):
        return pltpu.make_async_remote_copy(src_ref=src, dst_ref=dst, send_sem=ss, recv_sem=rs,
                                            device_id=to, device_id_type=MESH)

    loads = []
    for s in range(steps):
        for f, ref in enumerate((m_ref, fx_ref, fy_ref)):
            loads.append(pltpu.make_async_copy(
                ref.at[pl.ds(s * nlon, nlon)], dyn.at[s * n_lev + z, pl.ds(f * nlon, nlon)], in_sem.at[len(loads)]))
            loads[-1].start()
    load_x = pltpu.make_async_copy(x_hbm, x_ref, in_sem.at[len(loads)])
    load_x.start()

    def pack_x(s, src):
        def body(lev, _):
            for c in range(H):
                to = pl.ds(pl.multiple_of((lev * H + c) * SUB, SUB), SUB)
                hxo[s, 0, to, :] = src[pl.ds(lev * nlon + c, SUB, stride=nl), :]
                hxo[s, 1, to, :] = src[pl.ds(lev * nlon + nlon - H + c, SUB, stride=nl), :]
            return 0
        lax.fori_loop(0, n_lev, body, 0, unroll=True)

    for copy in loads:
        copy.wait()
    for s in range(steps):
        own = s * n_lev + z
        eout[s * 4:s * 4 + 1, :] = dyn[own, nlon - 1:nlon, :]
        eout[s * 4 + 1:s * 4 + 2, :] = dyn[own, 0:1, :]
        eout[s * 4 + 2:s * 4 + 3, :] = dyn[own, nlon:nlon + 1, :]
        eout[s * 4 + 3:s * 4 + 4, :] = dyn[own, nlon:nlon + 1, :]
    mp[0:SUB, :] = jnp.ones((SUB, LANES), jnp.float32)
    fp[nlon:nlon + SUB, :] = jnp.zeros((SUB, LANES), jnp.float32)
    load_x.wait()
    pack_x(0, x_ref)
    pl.semaphore_wait(barrier, len(who))

    pending = []

    def go(copy):
        copy.start()
        pending.append(copy)

    go(remote(eout, ein.at[1], ea_s.at[0], ea_r.at[1], {"gx": left}))
    go(remote(eout, ein.at[0], ea_s.at[1], ea_r.at[0], {"gx": right}))

    def send_dyn(s):
        for d, p in enumerate(peers):
            go(remote(dyn.at[s * n_lev + z], dyn.at[s * n_lev + z], d_s.at[s, d], d_r.at[s, z], {"tracer": p}))

    def send_x(s):
        go(remote(hxo.at[s, 0], hxi.at[s, 1], hx_s.at[s, 0], hx_r.at[s, 1], {"gx": left}))
        go(remote(hxo.at[s, 1], hxi.at[s, 0], hx_s.at[s, 1], hx_r.at[s, 0], {"gx": right}))

    send_x(0)
    send_dyn(0)

    def share_edges():
        for side in range(2):
            remote(eout, ein.at[side], ea_s.at[side], ea_r.at[side], {"gx": left}).wait_recv()
        for s in range(steps):
            edge[z, s * 4:s * 4 + 1, :] = ein[0, s * 4:s * 4 + 1, :]
            edge[z, s * 4 + 1:s * 4 + 4, :] = ein[1, s * 4 + 1:s * 4 + 4, :]
        for d, p in enumerate(peers):
            go(remote(edge.at[z], edge.at[z], eb_s.at[d], eb_r.at[z], {"tracer": p}))

    for s in range(steps):
        src = x_ref if s == 0 else xs
        dst = xs if s < steps - 1 else o_ref

        def x_inner(j, _):
            lev = lax.rem(z + j, n_lev)
            slot = s * n_lev + lev

            def here():
                remote(dyn.at[slot], dyn.at[slot], d_s.at[s, 0], d_r.at[s, lev], {"tracer": z}).wait_recv()
            if s > 0:
                pl.when(j > 0)(here)
            elif not isinstance(j, int):
                here()

            m = dyn[slot, 0:nlon, :]
            mp[SUB:SUB + nlon, :] = m
            fp[0:nlon, :] = dyn[slot, nlon:2 * nlon, :]
            f = fp[0:nlon, :]
            pw, qw = face_weights(f, mp[SUB - 1:SUB - 1 + nlon, :], m)
            cf[lev, 0:nlon, :] = f
            cp[lev, 0:nlon, :] = pw
            cq[lev, 0:nlon, :] = qw
            mx = m - (fp[1:nlon + 1, :] - f)
            inv = 1.0 / mx
            ca[lev] = m * inv
            cb[lev] = inv
            mxs[pl.ds(pl.multiple_of(lev * nlon, nlon), nlon), :] = mx
            base = lev * nlon
            sweep(
                lambda i: src[pl.ds(base + i, SUB, stride=nl), :],
                lambda k: (cf[lev, k:k + 1, :], cp[lev, k:k + 1, :], cq[lev, k:k + 1, :]),
                lambda i: (ca[lev, i:i + 1, :], cb[lev, i:i + 1, :]),
                functools.partial(put_x, base), H, nlon - H)
            return 0

        def put_x(base, i, v):
            qx[pl.ds(base + i, SUB, stride=nl), :] = v

        if s == 0:
            x_inner(0, 0)
            share_edges()
            lax.fori_loop(1, n_lev, x_inner, 0)

            def edge_here(j, _):
                lev = lax.rem(z + j, n_lev)
                remote(edge.at[lev], edge.at[lev], eb_s.at[0], eb_r.at[lev], {"tracer": z}).wait_recv()
                return 0
            lax.fori_loop(1, n_lev, edge_here, 0)
            for later in range(1, steps):
                send_dyn(later)
        else:
            lax.fori_loop(0, n_lev, x_inner, 0)
        for side in range(2):
            remote(hxo.at[s, 0], hxi.at[s, side], hx_s.at[s, side], hx_r.at[s, side], {"gx": left}).wait_recv()

        def x_edge(lev, _):
            base = lev * nlon
            slot = s * n_lev + lev
            first = slice(nlon, nlon + 1)
            m_w = edge[lev, s * 4:s * 4 + 1, :]
            m_e = edge[lev, s * 4 + 1:s * 4 + 2, :]
            f_e = edge[lev, s * 4 + 2:s * 4 + 3, :]
            f_w = dyn[slot, first, :]
            pw, qw = face_weights(f_w, m_w, dyn[slot, 0:1, :])
            cp[lev, 0:1, :] = pw
            cq[lev, 0:1, :] = qw
            m_last = dyn[slot, nlon - 1:nlon, :]
            pw, qw = face_weights(f_e, m_last, m_e)
            cf[lev, first, :] = f_e
            cp[lev, first, :] = pw
            cq[lev, first, :] = qw
            mx = m_last - (f_e - dyn[slot, 2 * nlon - 1:2 * nlon, :])
            inv = 1.0 / mx
            ca[lev, nlon - 1:nlon, :] = m_last * inv
            cb[lev, nlon - 1:nlon, :] = inv
            mxs[pl.ds(base + nlon - 1, 1), :] = mx

            def q(i):
                if i < 0:
                    return hxi[s, 0, pl.ds(pl.multiple_of((lev * H + i + H) * SUB, SUB), SUB), :]
                if i >= nlon:
                    return hxi[s, 1, pl.ds(pl.multiple_of((lev * H + i - nlon) * SUB, SUB), SUB), :]
                return src[pl.ds(base + i, SUB, stride=nl), :]

            for a, b in ((0, H), (nlon - H, nlon)):
                sweep(
                    q,
                    lambda k: (cf[lev, k:k + 1, :], cp[lev, k:k + 1, :], cq[lev, k:k + 1, :]),
                    lambda i: (ca[lev, i:i + 1, :], cb[lev, i:i + 1, :]),
                    functools.partial(put_x, base), a, b)
            return 0

        lax.fori_loop(0, n_lev, x_edge, 0, unroll=True)

        off = H * SUB

        mt = jnp.transpose(mxs[...])
        ft = jnp.transpose(jnp.concatenate(
            [dyn[s * n_lev + lev, 2 * nlon:3 * nlon, :] for lev in range(n_lev)], axis=0))
        myp[SUB:SUB + LANES, :] = mt
        fyp[0:LANES, :] = ft

        def turn(t, _):
            yb[pl.ds(off + t, LANES, stride=SUB), :] = jnp.transpose(qx[t * nl:(t + 1) * nl, :])
        for t in range(SUB):
            turn(t, 0)
        extra = jnp.concatenate([mt[0:1], mt[LANES - 1:LANES], ft[0:1], ft[0:1], ft[0:1], ft[0:1], ft[0:1], ft[0:1]], axis=0)
        for side in range(2):
            hyo[s, side, H * SUB:(H + 1) * SUB, :] = extra
        hyo[s, 0, 0:H * SUB, :] = yb[off:off + H * SUB, :]
        hyo[s, 1, 0:H * SUB, :] = yb[off + (LANES - H) * SUB:off + LANES * SUB, :]
        go(remote(hyo.at[s, 0], hyi.at[s, 1], hy_s.at[s, 0], hy_r.at[s, 1], {"gy": south}))
        go(remote(hyo.at[s, 1], hyi.at[s, 0], hy_s.at[s, 1], hy_r.at[s, 0], {"gy": north}))

        f = fyp[SUB:LANES, :]
        pw, qw = face_weights(f, myp[2 * SUB - 1:SUB + LANES - 1, :], myp[2 * SUB:SUB + LANES, :])
        yp[SUB:LANES, :] = pw
        yq[SUB:LANES, :] = qw
        m = myp[SUB:LANES, :]
        inv = 1.0 / (m - (fyp[1:LANES - SUB + 1, :] - fyp[0:LANES - SUB, :]))
        ya[0:LANES - SUB, :] = m * inv
        ybt[0:LANES - SUB, :] = inv

        def y_rows(first, count):
            sweep(
                lambda i: yb[pl.ds(pl.multiple_of(off + (first + i) * SUB, SUB), SUB), :],
                lambda k: (fyp[pl.ds(first + k, 1), :], yp[pl.ds(first + k, 1), :], yq[pl.ds(first + k, 1), :]),
                lambda i: (ya[pl.ds(first + i, 1), :], ybt[pl.ds(first + i, 1), :]),
                put_y(first), 0, count)

        def put_y(first):
            def put(i, v):
                yo[pl.ds(pl.multiple_of((first + i) * SUB, SUB), SUB), :] = v
            return put

        def y_inner(b, _):
            y_rows(SUB + b * 16, 16)
            return 0
        lax.fori_loop(0, (LANES - 2 * SUB) // 16, y_inner, 0)

        for side in range(2):
            remote(hyo.at[s, 0], hyi.at[s, side], hy_s.at[s, side], hy_r.at[s, side], {"gy": south}).wait_recv()
        at_south, at_north = gy == 0, gy == n_y - 1
        yb[0:H * SUB, :] = jnp.where(at_south, 0.0, hyi[s, 0, 0:H * SUB, :])
        yb[off + LANES * SUB:off + (LANES + H) * SUB, :] = jnp.where(at_north, 0.0, hyi[s, 1, 0:H * SUB, :])
        e = H * SUB
        myp[0:SUB, :] = jnp.broadcast_to(jnp.where(at_south, 1.0, hyi[s, 0, e + 1:e + 2, :]), (SUB, LANES))
        myp[SUB + LANES:2 * SUB + LANES, :] = jnp.broadcast_to(
            jnp.where(at_north, 1.0, hyi[s, 1, e:e + 1, :]), (SUB, LANES))
        fyp[LANES:LANES + SUB, :] = jnp.broadcast_to(
            jnp.where(at_north, 0.0, hyi[s, 1, e + 2:e + 3, :]), (SUB, LANES))
        fyp[0:1, :] = jnp.where(at_south, 0.0, fyp[0:1, :])
        for a in (0, LANES):
            f = fyp[a:a + SUB, :]
            pw, qw = face_weights(f, myp[a + SUB - 1:a + 2 * SUB - 1, :], myp[a + SUB:a + 2 * SUB, :])
            yp[a:a + SUB, :] = pw
            yq[a:a + SUB, :] = qw
        for a in (0, LANES - SUB):
            m = myp[a + SUB:a + 2 * SUB, :]
            inv = 1.0 / (m - (fyp[a + 1:a + SUB + 1, :] - fyp[a:a + SUB, :]))
            ya[a:a + SUB, :] = m * inv
            ybt[a:a + SUB, :] = inv

        def y_edge(b, _):
            y_rows(b * (LANES - SUB), SUB)
            return 0
        lax.fori_loop(0, 2, y_edge, 0, unroll=True)

        def back(t, _):
            dst[t * nl:(t + 1) * nl, :] = jnp.transpose(yo[pl.ds(t, LANES, stride=SUB), :])
        for t in range(SUB):
            back(t, 0)
        if s < steps - 1:
            pack_x(s + 1, xs)
            send_x(s + 1)

    for copy in pending:
        copy.wait_send()


def on_device(tracers, air_mass, flux_x, flux_y):
    nt, nlev, nlon, nlat = tracers.shape
    steps, tl = air_mass.shape[:2]
    n_lev, n_x, n_y = lax.axis_size("tracer"), lax.axis_size("gx"), lax.axis_size("gy")
    assert nt == SUB and nlat == LANES and nlev * nlon == LANES and tl == 1 and steps * 4 <= SUB
    rows = nt * nlev * nlon
    V = lambda *shape: pltpu.VMEM(shape, jnp.float32)
    dma = lambda *shape: pltpu.SemaphoreType.DMA(shape)
    H = 3
    out = pl.pallas_call(
        functools.partial(kernel, n_lev, n_x, n_y, steps, tl, nlon),
        out_shape=jax.ShapeDtypeStruct((rows, LANES), jnp.float32),
        in_specs=[pl.BlockSpec(memory_space=pltpu.HBM)] * 4,
        out_specs=pl.BlockSpec(memory_space=pltpu.VMEM),
        scratch_shapes=[
            V(rows, LANES), dma(3 * steps + 1),
            V(steps * n_lev, 3 * nlon, LANES),
            V(SUB, LANES), V(2, SUB, LANES), V(n_lev, SUB, LANES),
            V(steps, 2, n_lev * H * SUB, LANES), V(steps, 2, n_lev * H * SUB, LANES),
            V(steps, 2, (H + 1) * SUB, LANES), V(steps, 2, (H + 1) * SUB, LANES),
            V(rows, LANES), V(rows, LANES), V((LANES + 2 * H) * SUB, LANES), V(LANES * SUB, LANES),
            V(n_lev, nlon + SUB, LANES), V(n_lev, nlon + SUB, LANES), V(n_lev, nlon + SUB, LANES),
            V(n_lev, nlon, LANES), V(n_lev, nlon, LANES),
            V(nlon + 2 * SUB, LANES), V(nlon + SUB, LANES), V(LANES, LANES),
            V(LANES + 2 * SUB, LANES), V(LANES + SUB, LANES), V(LANES + SUB, LANES), V(LANES + SUB, LANES),
            V(LANES, LANES), V(LANES, LANES),
            dma(steps, n_lev), dma(steps, n_lev), dma(2), dma(2), dma(n_lev), dma(n_lev),
            dma(steps, 2), dma(steps, 2), dma(steps, 2), dma(steps, 2),
        ],
        compiler_params=pltpu.CompilerParams(
            collective_id=0, has_side_effects=True, vmem_limit_bytes=56 * 1024 * 1024),
    )(tracers.reshape(rows, LANES), air_mass.reshape(-1, LANES), flux_x.reshape(-1, LANES), flux_y.reshape(-1, LANES))
    return out.reshape(tracers.shape)


def solution(mesh):
    in_specs = (
        P("tracer", None, "gx", "gy"),
        P(None, "tracer", "gx", "gy"),
        P(None, "tracer", "gx", "gy"),
        P(None, "tracer", "gx", "gy"),
    )
    out_specs = P("tracer", None, "gx", "gy")
    return jax.shard_map(
        on_device, mesh=mesh, in_specs=in_specs, out_specs=out_specs, check_vma=False
    )
```
